256 devices in a mesh: node: 128 (over z, y, x), row: 2 (over core).
Axes of the slice: x: 4, y: 4, z: 8, core: 2. Of those that a mesh axis runs over, the one named last changes fastest.
Arguments:
- root_inv_t: float32 [3072, 3072], P('node', 'row'), as said below
- child_inv_t: float32 [5120, 5120], P('node', 'row'), as said below
- panel_t: float32 [5120, 3072], P('node', 'row'), may hold values from -0.109375 to 0.109375
- deriv_t: float32 [5120, 3072], P('node', 'row'), may hold values from -0.0029296875 to 0.0029296875
- pattern: int32 [24], replicated, may hold values 0 or 1
- owner: int32 [24], replicated, may hold values from 0 to 3
Outputs:
- root_cov: float32 [3072, 3072], P('node', 'row')
- coupling: float32 [5120, 3072], P('node', 'row')
- child_cov: float32 [5120, 5120], P('node', 'row')
- grad: float32 [4], replicated
The draws below stay inside these ranges and needn't reach their ends.
Inputs may be any that keep to these rules, and one draw needn't show every extreme that they name: `root_inv_t`: upper triangular with positive diagonal. `child_inv_t`: upper triangular with positive diagonal.
All inputs are finite; a program needn't handle non-finite values.
Results may differ from the reference program's by a relative error of at most 0.00019.
Values sent between devices are 32-bit elements; how exact they have to be, the bound alone decides.
No kernel may reach another device: no remote copies, remote signals or barrier semaphores. Data moves between devices by JAX's collectives and lax.ppermute only.
A program may use at most 256 MiB of HBM per device.

```python
import jax
import jax.numpy as jnp
from jax import lax

SR = 3072
SC = 5120
NHYP = 4
NB = 24


def upper_factor(key, order, spread, low, high):
    rows = jnp.arange(order)[:, None]
    cols = jnp.arange(order)[None, :]
    first, second = jax.random.split(key)
    offdiag = jax.random.normal(first, (order, order), jnp.float32) * spread
    diagonal = jax.random.uniform(second, (order, order), jnp.float32, low, high)
    return jnp.where(cols > rows, offdiag, jnp.where(cols == rows, diagonal, 0.0))


def draw_root_inv_t(key, part):
    key = jax.random.fold_in(key, 11)
    return upper_factor(key, SR, 1.0 / SR ** 0.5, 0.6, 1.4)


def draw_child_inv_t(key, part):
    key = jax.random.fold_in(key, 23)
    return upper_factor(key, SC, 1.0 / SC ** 0.5, 0.6, 1.4)


def with_ends(array, stream_key, low, largest):
    longest = array.shape.index(max(array.shape))
    spots = []
    for shift in (0, 1):
        where = [jax.random.randint(jax.random.fold_in(stream_key, axis), (), 0, length) for axis, length in enumerate(array.shape)]
        where[longest] = (where[longest] + shift) % array.shape[longest]
        spots.append(tuple(where))
    return array.at[spots[0]].set(low).at[spots[1]].set(largest)


def shard_levels(rng, dims, cuts, least, top_value):
    factor_of, own = 1.0, jax.random.fold_in(rng, 6)
    for axis_at, shards_of in cuts:
        steps = jnp.exp(jax.random.uniform(jax.random.fold_in(own, axis_at), (shards_of,), jnp.float32, least / len(cuts), top_value / len(cuts)))
        factor_of = factor_of * jnp.repeat(steps, dims[axis_at] // shards_of).reshape([-1 if axis == axis_at else 1 for axis in range(len(dims))])
    return factor_of


def bell_draw(stream_key, extent, scale, bound, cuts=(), kind=jnp.bfloat16):
    entries = jax.random.normal(stream_key, extent, jnp.float32) * scale
    if len(cuts) > 0:
        entries = shard_levels(stream_key, extent, cuts, -0.22, 0.18) * entries
    return jnp.clip(entries, min=-bound, max=bound).astype(kind)


def setup_inputs(seed: int = 0) -> dict:
    key_list = jax.random.split(jax.random.key(seed), 7)
    return {
        "root_inv_t": draw_root_inv_t(jax.random.fold_in(key_list[6], 71), 0),
        "child_inv_t": draw_child_inv_t(jax.random.fold_in(key_list[6], 71), 0),
        "panel_t": bell_draw(key_list[2], (SC, SR), SR ** -0.5, 0.109375, ((0, 128), (1, 2)), jnp.float32),
        "deriv_t": bell_draw(key_list[3], (SC, SR), (SR * SC // NHYP) ** -0.5, 0.0029296875, ((0, 128), (1, 2)), jnp.float32),
        "pattern": with_ends((jax.random.randint(key_list[4], (NB,), 0, 4) < 3).astype(jnp.int32), jax.random.fold_in(key_list[4], 1), 0, 1),
        "owner": with_ends(jax.random.randint(key_list[5], (NB,), 0, NHYP), jax.random.fold_in(key_list[5], 1), 0, NHYP - 1).astype(jnp.int32),
    }


def reference(root_inv_t, child_inv_t, panel_t, deriv_t, pattern, owner):
    highest = lax.Precision.HIGHEST
    block = SR // NB
    col_mask = jnp.broadcast_to(pattern.astype(jnp.float32)[:, None], (NB, block)).reshape(SR)
    panel_m = panel_t * col_mask[None, :]
    root_cov = jnp.dot(root_inv_t, root_inv_t.T, precision=highest, preferred_element_type=jnp.float32)
    coupling = -jnp.dot(panel_m, root_cov, precision=highest, preferred_element_type=jnp.float32) * col_mask[None, :]
    child_cov = jnp.dot(child_inv_t, child_inv_t.T, precision=highest, preferred_element_type=jnp.float32)
    child_cov = child_cov - jnp.dot(coupling, panel_m.T, precision=highest, preferred_element_type=jnp.float32)
    col_sums = jnp.sum(coupling * deriv_t, axis=0)
    block_sums = jnp.sum(col_sums.reshape(NB, block), axis=1)
    onehot = (owner[None, :] == jnp.arange(NHYP, dtype=jnp.int32)[:, None]).astype(jnp.float32)
    grad = 2.0 * jnp.sum(onehot * block_sums[None, :], axis=1)
    return root_cov, coupling, child_cov, grad
```

```python
import jax
import jax.numpy as jnp
from jax import lax
from jax.sharding import PartitionSpec as P

NHYP = 4
NZ, NY, NX = 8, 4, 4
NODES = [(z, y, x) for z in range(NZ) for y in range(NY) for x in range(NX)]


def node_id(z, y, x):
    return ((z % NZ) * NY + y % NY) * NX + x % NX


def shift(a, dz=0, dy=0, dx=0):
    perm = [(node_id(z, y, x), node_id(z + dz, y + dy, x + dx)) for z, y, x in NODES]
    return lax.ppermute(a, "node", perm)


def swap_core(a):
    return lax.ppermute(a, "row", [(0, 1), (1, 0)])


def dot_bt(a, b):
    return lax.dot_general(
        a,
        b,
        (((1,), (1,)), ((), ())),
        precision=lax.Precision.HIGH,
        preferred_element_type=jnp.float32,
    )


def place(chunks, axis):
    size = len(chunks)
    shape = list(chunks[0][1].shape)
    shape.insert(axis, size)
    out = jnp.zeros(shape, chunks[0][1].dtype)
    for index, chunk in chunks:
        out = lax.dynamic_update_index_in_dim(out, chunk, index, axis)
    return out


def gather_z(a, z, sign=1):
    chunks = [(z, a)]
    up, down = a, a
    for k in range(1, 5):
        up = shift(up, dz=sign)
        chunks.append((lax.rem(z - sign * k + NZ, NZ), up))
        if k < 4:
            down = shift(down, dz=-sign)
            chunks.append((lax.rem(z + sign * k + NZ, NZ), down))
    return place(chunks, 0)


def gather_line(a, at, axis, where):
    chunks = [(at, a)]
    for k in (1, 3, 2):
        chunks.append((lax.rem(at - k + 4, 4), shift(a, **{axis: k})))
    return place(chunks, where)


def gather_plane(a, y, x, first="x"):
    if first == "x":
        return gather_line(gather_line(a, x, "dx", 0), y, "dy", 0)
    return gather_line(gather_line(a, y, "dy", 0), x, "dx", 1)


def reduce_core(a, core):
    half = a.shape[0] // 2
    mine = lax.dynamic_slice_in_dim(a, core * half, half)
    other = lax.dynamic_slice_in_dim(a, (1 - core) * half, half)
    return mine + swap_core(other)


def all_sum(v, core_too=True):
    v = v + swap_core(v)
    for k in (1, 2, 4):
        v = v + shift(v, dz=k)
    for axis in ("dy", "dx"):
        parts = [shift(v, **{axis: k}) for k in (1, 3, 2)]
        v = v + parts[0] + parts[1] + parts[2]
    return v


def per_device(root_inv_t, child_inv_t, panel_t, deriv_t, pattern, owner):
    node, core = lax.axis_index("node"), lax.axis_index("row")
    z, y, x = node // (NY * NX), lax.rem(node // NX, NY), lax.rem(node, NX)
    plane = lax.rem(node, NY * NX)
    rows_r, half = root_inv_t.shape
    rows_c, half_c = child_inv_t.shape
    sr, sc = 2 * half, 2 * half_c
    width = sr // pattern.shape[0]
    mask_all = jnp.repeat(pattern.astype(jnp.float32), width)
    owner_all = jnp.repeat(owner, width)
    mask = lax.dynamic_slice_in_dim(mask_all, core * half, half)
    owner_cols = lax.dynamic_slice_in_dim(owner_all, core * half, half)
    panel_m = panel_t * mask[None, :]
    zc = sr // NZ
    mask_z = lax.dynamic_slice_in_dim(mask_all, z * zc, zc)

    r_z = gather_z(root_inv_t, z).reshape(NZ * rows_r, half)
    h = half // 2
    r_p1 = gather_plane(root_inv_t[:, :h], y, x, "x").reshape(16 * rows_r, h)
    r_p2 = gather_plane(root_inv_t[:, h:], y, x, "y").reshape(16 * rows_r, h)
    s_part = dot_bt(r_z[:, :h], r_p1) + dot_bt(r_z[:, h:], r_p2)
    s_own = reduce_core(s_part, core)
    s4 = s_own.reshape(4, rows_r, zc)
    s_a = gather_plane(s4[:2], y, x, "x")
    s_b = gather_plane(s4[2:], y, x, "y")
    s_all = jnp.concatenate([s_a, s_b], axis=2)
    s_all = s_all.transpose(2, 0, 1, 3, 4).reshape(half, zc)
    root_cov = lax.dynamic_slice_in_dim(s_all, plane * rows_r, rows_r, axis=1).T

    p_z = gather_z(panel_m, z, -1).reshape(NZ * rows_c, half)
    c_part = jnp.dot(
        p_z, s_all, precision=lax.Precision.HIGH, preferred_element_type=jnp.float32
    )
    c_own = -reduce_core(c_part, core) * mask_z[None, :]
    c_all = gather_z(c_own, z)
    c_rows = lax.dynamic_slice_in_dim(c_all, lax.rem(z, 4) * rows_c, rows_c, axis=1)
    c_rows = c_rows.transpose(1, 0, 2).reshape(rows_c, 2, half)
    c_mine = lax.dynamic_index_in_dim(c_rows, core, 1, keepdims=False)
    c_other = lax.dynamic_index_in_dim(c_rows, 1 - core, 1, keepdims=False)
    c_other = swap_core(c_other)
    coupling = jnp.where(z // 4 == core, c_mine, c_other)

    k_p = gather_plane(child_inv_t, y, x, "y").reshape(16 * rows_c, half_c)
    k_z = gather_z(child_inv_t, z, -1).reshape(NZ * rows_c, half_c)
    kk = reduce_core(dot_bt(k_z, k_p), core)
    p_p = gather_plane(panel_m, y, x, "x").reshape(16 * rows_c, half)
    p_o = swap_core(p_p)
    p_lo = jnp.where(core == 0, p_p, p_o)
    p_hi = jnp.where(core == 0, p_o, p_p)
    c_k = c_all.transpose(1, 0, 2).reshape(4 * rows_c, sr)
    block = kk - dot_bt(c_k[:, :half], p_lo) - dot_bt(c_k[:, half:], p_hi)
    send = block.T.reshape(16, rows_c, 4 * rows_c)
    groups = [[zz * 16 + i for i in range(16)] for zz in range(NZ)]
    got = lax.all_to_all(send, "node", 0, 0, axis_index_groups=groups, tiled=True)
    child_cov = got.reshape(16, rows_c, 4, rows_c).transpose(1, 2, 0, 3).reshape(rows_c, half_c)

    col_sums = jnp.sum(coupling * deriv_t, axis=0)
    onehot = (owner_cols[None, :] == jnp.arange(NHYP, dtype=jnp.int32)[:, None]).astype(jnp.float32)
    partial_grad = jnp.sum(onehot * col_sums[None, :], axis=1)
    grad = 2.0 * all_sum(partial_grad)
    return (root_cov, coupling, child_cov, grad)


def solution(mesh):
    placed = (P("node", "row"), P("node", "row"), P("node", "row"), P("node", "row"), P(), P())
    return jax.shard_map(
        per_device,
        mesh=mesh,
        in_specs=placed,
        out_specs=(P("node", "row"), P("node", "row"), P("node", "row"), P()),
        check_vma=False,
    )
```

```python
import functools

import jax
import jax.numpy as jnp
from jax import lax
from jax.experimental import pallas as pl
from jax.experimental.pallas import tpu as pltpu
from jax.sharding import PartitionSpec as P

NHYP = 4
NZ, NY, NX = 8, 4, 4
NODES = [(z, y, x) for z in range(NZ) for y in range(NY) for x in range(NX)]
PLANES = [[z * NY * NX + i for i in range(NY * NX)] for z in range(NZ)]
VMEM = pl.BlockSpec(memory_space=pltpu.VMEM)
SMEM = pl.BlockSpec(memory_space=pltpu.SMEM)
F32, BF16 = jnp.float32, jnp.bfloat16


def node_id(z, y, x):
    return ((z % NZ) * NY + y % NY) * NX + x % NX


def shift(a, dz=0, dy=0, dx=0):
    perm = [(node_id(z, y, x), node_id(z + dz, y + dy, x + dx)) for z, y, x in NODES]
    return lax.ppermute(a, "node", perm)


def swap_core(a):
    return lax.ppermute(a, "row", [(0, 1), (1, 0)])


RING = (0, 1, 7, 2, 6, 3, 5, 4)
LINE = (0, 1, 3, 2)


def ring_z(a):
    chunks = [a]
    up, down = a, a
    for k in range(1, 5):
        up = shift(up, dz=1)
        chunks.append(up)
        if k < 4:
            down = shift(down, dz=-1)
            chunks.append(down)
    return chunks


def line(a, axis):
    return [a] + [shift(a, **{axis: k}) for k in LINE[1:]]


def plane_xy(a):
    return line(jnp.stack(line(a, "dx")), "dy")


def plane_yx(a):
    return line(jnp.stack(line(a, "dy")), "dx")


def halves(x):
    hi = x.astype(BF16)
    return hi, (x - hi.astype(F32)).astype(BF16)


def dot3(a, b, dims):
    d = functools.partial(
        lax.dot_general, dimension_numbers=(dims, ((), ())), preferred_element_type=F32
    )
    return d(a[0], b[0]) + (d(a[0], b[1]) + d(a[1], b[0]))


NT, NN = ((1,), (1,)), ((1,), (0,))


def call(body, ins, outs, scratch, flops, name):
    vmem = sum(a.size * a.dtype.itemsize for a in ins) + sum(4 * o[0] * o[1] for o in outs)
    vmem += sum(s.dtype.itemsize * functools.reduce(lambda p, q: p * q, s.shape) for s in scratch)
    return pl.pallas_call(
        body,
        out_shape=[jax.ShapeDtypeStruct(o, F32) for o in outs],
        in_specs=[SMEM] + [VMEM] * (len(ins) - 1),
        out_specs=[VMEM] * len(outs),
        scratch_shapes=scratch,
        cost_estimate=pl.CostEstimate(flops=flops, bytes_accessed=vmem // 2, transcendentals=0),
        compiler_params=pltpu.CompilerParams(vmem_limit_bytes=min(56 << 20, 2 * vmem + (8 << 20))),
        name=name,
    )(*ins)


def wrap(v, n):
    return lax.rem(v + n, n)


def split_rows(full, core, mine, other):
    h = mine.shape[0]
    mine[...] = full[pl.ds(pl.multiple_of(core * h, 8), h), :]
    other[...] = full[pl.ds(pl.multiple_of((1 - core) * h, 8), h), :]


def root_body(idx, *refs):
    rz, pa, pb, mine, other, fz, fp, full = refs[:8], refs[8:12], refs[12:16], *refs[16:]
    z, y, x, core = idx[0], idx[1], idx[2], idx[3]
    n, h = rz[0].shape[0], rz[0].shape[1] // 2
    for k in range(8):
        fz[pl.ds(pl.multiple_of(wrap(z - RING[k], 8) * n, 8), n), :] = rz[k][...]
    for j in range(4):
        for i in range(4):
            at = (wrap(y - LINE[j], 4) * 4 + wrap(x - LINE[i], 4)) * n
            fp[pl.ds(pl.multiple_of(at, 8), n), :h] = pa[j][i]
            at = (wrap(y - LINE[i], 4) * 4 + wrap(x - LINE[j], 4)) * n
            fp[pl.ds(pl.multiple_of(at, 8), n), h:] = pb[j][i]
    full[...] = dot3(halves(fz[...]), halves(fp[...]), NT)
    split_rows(full, core, mine, other)


def couple_body(idx, *refs):
    pz, sa, sb, mine, other, s_all, fz, full = refs[:8], refs[8:12], refs[12:16], *refs[16:]
    z, y, x, core = idx[0], idx[1], idx[2], idx[3]
    n, m = pz[0].shape[0], sa[0].shape[2]
    for k in range(8):
        fz[pl.ds(pl.multiple_of(wrap(z - RING[k], 8) * n, 8), n), :] = pz[k][...]
    for j in range(4):
        for i in range(4):
            for zz in range(2):
                at = ((zz * 4 + wrap(y - LINE[j], 4)) * 4 + wrap(x - LINE[i], 4)) * m
                s_all[pl.ds(pl.multiple_of(at, 8), m), :] = sa[j][i, zz]
                at = ((zz * 4 + 8 + wrap(y - LINE[i], 4)) * 4 + wrap(x - LINE[j], 4)) * m
                s_all[pl.ds(pl.multiple_of(at, 8), m), :] = sb[j][i, zz]
    full[...] = dot3(halves(fz[...]), halves(s_all[...]), NN)
    split_rows(full, core, mine, other)


def factor_body(idx, *refs):
    kz, kp, mine, other, fz, full = refs[:8], *refs[8:]
    z, core = idx[0], idx[3]
    n = kz[0].shape[0]
    for k in range(8):
        fz[pl.ds(pl.multiple_of(wrap(z - RING[k], 8) * n, 8), n), :] = kz[k][...]
    full[...] = dot3(halves(fz[...]), halves(kp[...]), NT)
    split_rows(full, core, mine, other)


def child_body(idx, *refs):
    cz, p_mine, p_other, kk, out, hi, lo = refs[:8], *refs[8:]
    z, core = idx[0], idx[3]
    w = cz[0].shape[1]
    for part, src in ((core, p_mine), (1 - core, p_other)):
        for b in range(4):
            a, c = halves(src[:, b * w : (b + 1) * w])
            hi[part * 4 + b] = a
            lo[part * 4 + b] = c
    out[...] = kk[...]
    for k in range(8):
        at = wrap(z - RING[k], 8)
        out[...] -= dot3((hi[at], lo[at]), halves(cz[k][...]), NT)


def all_sum(v):
    v = v + swap_core(v)
    for k in (1, 2, 4):
        v = v + shift(v, dz=k)
    for axis in ("dy", "dx"):
        parts = [shift(v, **{axis: k}) for k in (1, 3, 2)]
        v = v + parts[0] + parts[1] + parts[2]
    return v


def per_device(root_inv_t, child_inv_t, panel_t, deriv_t, pattern, owner):
    node, core = lax.axis_index("node"), lax.axis_index("row")
    z, y, x = node // (NY * NX), lax.rem(node // NX, NY), lax.rem(node, NX)
    plane = lax.rem(node, NY * NX)
    idx = jnp.stack([z, y, x, core]).astype(jnp.int32)
    rr, half = root_inv_t.shape
    rc, half_c = child_inv_t.shape
    sr = 2 * half
    width = sr // pattern.shape[0]
    mask_all = jnp.repeat(pattern.astype(F32), width)
    owner_all = jnp.repeat(owner, width)
    mask = lax.dynamic_slice_in_dim(mask_all, core * half, half)
    owner_cols = lax.dynamic_slice_in_dim(owner_all, core * half, half)
    panel_m = panel_t * mask[None, :]
    zc = sr // NZ
    mask_z = lax.dynamic_slice_in_dim(mask_all, z * zc, zc)

    wide = lax.all_gather(
        jnp.concatenate([child_inv_t, panel_m], axis=1),
        "node",
        axis=0,
        tiled=True,
        axis_index_groups=PLANES,
    )

    h = half // 2
    r_z = ring_z(root_inv_t)
    r_a = plane_xy(root_inv_t[:, :h])
    r_b = plane_yx(root_inv_t[:, h:])
    mine, other = call(
        root_body,
        [idx, *r_z, *r_a, *r_b],
        [(NZ * rr // 2, zc)] * 2,
        [pltpu.VMEM((NZ * rr, half), F32), pltpu.VMEM((16 * rr, half), F32), pltpu.VMEM((NZ * rr, zc), F32)],
        6 * NZ * rr * 16 * rr * half,
        "root_cov",
    )
    s_own = (mine + swap_core(other)).reshape(4, rr, zc)
    s_a = plane_xy(s_own[:2])
    s_b = plane_yx(s_own[2:])

    panel_later, _ = lax.optimization_barrier((panel_m, r_z[-1]))
    p_z = ring_z(panel_later)
    mine, other, s_all = call(
        couple_body,
        [idx, *p_z, *s_a, *s_b],
        [(NZ * rc // 2, zc)] * 2 + [(half, zc)],
        [pltpu.VMEM((NZ * rc, half), F32), pltpu.VMEM((NZ * rc, zc), F32)],
        6 * NZ * rc * half * zc,
        "coupling",
    )
    c_own = -(mine + swap_core(other)) * mask_z[None, :]
    c_z = ring_z(c_own)
    root_cov = lax.dynamic_slice_in_dim(s_all, plane * rr, rr, axis=1).T

    child_later, _ = lax.optimization_barrier((child_inv_t, p_z[-1]))
    k_z = ring_z(child_later)
    mine, other = call(
        factor_body,
        [idx, *k_z, wide[:, :half_c]],
        [(NZ * rc // 2, 16 * rc)] * 2,
        [pltpu.VMEM((NZ * rc, half_c), F32), pltpu.VMEM((NZ * rc, 16 * rc), F32)],
        6 * NZ * rc * 16 * rc * half_c,
        "factor",
    )
    kk = (mine + swap_core(other)).T
    p_mine = wide[:, half_c:]
    p_other = swap_core(p_mine)
    (block,) = call(
        child_body,
        [idx, *c_z, p_mine, p_other, kk],
        [(16 * rc, 4 * rc)],
        [pltpu.VMEM((NZ, 16 * rc, zc), BF16)] * 2,
        6 * 16 * rc * 4 * rc * sr,
        "child_cov",
    )
    got = lax.all_to_all(
        block.reshape(16, rc, 4 * rc), "node", 0, 0, axis_index_groups=PLANES, tiled=True
    )
    child_cov = got.reshape(16, rc, 4, rc).transpose(1, 2, 0, 3).reshape(rc, half_c)

    def own_rows(target):
        parts = []
        for k in range(NZ):
            rows = lax.dynamic_slice_in_dim(c_z[k], lax.rem(z, 4) * rc, rc)
            parts.append(rows)
        out = jnp.zeros((rc, sr), F32)
        for k in range(NZ):
            out = lax.dynamic_update_slice_in_dim(out, parts[k], wrap(z - RING[k], 8) * zc, axis=1)
        return out

    c_rows = own_rows(core)
    c_mine = lax.dynamic_slice_in_dim(c_rows, core * half, half, axis=1)
    c_other = swap_core(lax.dynamic_slice_in_dim(c_rows, (1 - core) * half, half, axis=1))
    coupling = jnp.where(z // 4 == core, c_mine, c_other)

    col_sums = jnp.sum(coupling * deriv_t, axis=0)
    onehot = (owner_cols[None, :] == jnp.arange(NHYP, dtype=jnp.int32)[:, None]).astype(F32)
    partial_grad = jnp.sum(onehot * col_sums[None, :], axis=1)
    grad = 2.0 * all_sum(partial_grad)
    return (root_cov, coupling, child_cov, grad)


def solution(mesh):
    placed = (P("node", "row"), P("node", "row"), P("node", "row"), P("node", "row"), P(), P())
    return jax.shard_map(
        per_device,
        mesh=mesh,
        in_specs=placed,
        out_specs=(P("node", "row"), P("node", "row"), P("node", "row"), P()),
        check_vma=False,
    )
```

```python
import functools

import jax
import jax.numpy as jnp
from jax import lax
from jax.experimental import pallas as pl
from jax.experimental.pallas import tpu as pltpu
from jax.sharding import PartitionSpec as P

NHYP = 4
NZ, NY, NX = 8, 4, 4
NODES = [(z, y, x) for z in range(NZ) for y in range(NY) for x in range(NX)]
PLANES = [[z * NY * NX + i for i in range(NY * NX)] for z in range(NZ)]
VMEM = pl.BlockSpec(memory_space=pltpu.VMEM)
SMEM = pl.BlockSpec(memory_space=pltpu.SMEM)
F32, BF16 = jnp.float32, jnp.bfloat16


def node_id(z, y, x):
    return ((z % NZ) * NY + y % NY) * NX + x % NX


def shift(a, dz=0, dy=0, dx=0):
    perm = [(node_id(z, y, x), node_id(z + dz, y + dy, x + dx)) for z, y, x in NODES]
    return lax.ppermute(a, "node", perm)


def shift_cores(a, first, second):
    perm = []
    for z, y, x in NODES:
        for core, (dz, dy, dx) in enumerate((first, second)):
            perm.append((node_id(z, y, x) * 2 + core, node_id(z + dz, y + dy, x + dx) * 2 + core))
    return lax.ppermute(a, ("node", "row"), perm)


def swap_core(a):
    return lax.ppermute(a, "row", [(0, 1), (1, 0)])


RING = (0, 1, 7, 2, 6, 3, 5, 4)
LINE = (0, 1, 3, 2)


def after(a, *others):
    return lax.optimization_barrier((a, *others))[0]


def ring_z(a, late=()):
    late = dict(late)
    chunks = [a]
    up, down = a, a
    for k in range(1, 4):
        if k in late:
            up, down = lax.optimization_barrier((up, down, *late[k]))[:2]
        up = shift(up, dz=1)
        down = shift(down, dz=-1)
        chunks += [up, down]
    last = jnp.where(lax.axis_index("row") == 0, up, down)
    if 4 in late:
        last = after(last, *late[4])
    chunks.append(shift_cores(last, (1, 0, 0), (-1, 0, 0)))
    return chunks


def gather_plane(a):
    a = jnp.stack([a] + [shift_cores(a, (0, 0, k), (0, k, 0)) for k in LINE[1:]])
    return [a] + [shift_cores(a, (0, k, 0), (0, 0, k)) for k in LINE[1:]]


LINES = [[z * NY * NX + i for z in range(NZ)] for i in range(NY * NX)]


def exchange(blocks, groups):
    return lax.all_to_all(blocks, "node", 0, 0, axis_index_groups=groups, tiled=True)


def halves(x):
    hi = x.astype(BF16)
    return hi, (x - hi.astype(F32)).astype(BF16)


def dot3(a, b, dims):
    d = functools.partial(
        lax.dot_general, dimension_numbers=(dims, ((), ())), preferred_element_type=F32
    )
    return d(a[0], b[0]) + (d(a[0], b[1]) + d(a[1], b[0]))


NT, NN = ((1,), (1,)), ((1,), (0,))


def call(body, ins, outs, scratch, flops, name):
    outs = [o if hasattr(o, "dtype") else jax.ShapeDtypeStruct(o, F32) for o in outs]
    vmem = sum(a.size * a.dtype.itemsize for a in [*ins, *outs])
    vmem += sum(s.dtype.itemsize * functools.reduce(lambda p, q: p * q, s.shape) for s in scratch)
    return pl.pallas_call(
        body,
        out_shape=outs,
        in_specs=[SMEM] + [VMEM] * (len(ins) - 1),
        out_specs=[VMEM] * len(outs),
        scratch_shapes=scratch,
        cost_estimate=pl.CostEstimate(flops=flops, bytes_accessed=vmem // 2, transcendentals=0),
        compiler_params=pltpu.CompilerParams(vmem_limit_bytes=min(56 << 20, 2 * vmem + (8 << 20))),
        name=name,
    )(*ins)


def wrap(v, n):
    return lax.rem(v + n, n)


def split_rows(full, core, mine, other):
    h = mine.shape[0]
    mine[...] = full[pl.ds(pl.multiple_of(core * h, 8), h), :]
    other[...] = full[pl.ds(pl.multiple_of((1 - core) * h, 8), h), :]


def turn(a):
    return pltpu.roll(a, a.shape[-1] // 2, axis=a.ndim - 1)


def in_half(shape, core):
    return (lax.broadcasted_iota(jnp.int32, shape, len(shape) - 1) < shape[-1] // 2) == (core == 0)


def plane_at(idx, j, i):
    y, x, core = idx[1], idx[2], idx[3]
    dy = jnp.where(core == 0, LINE[j], LINE[i])
    dx = jnp.where(core == 0, LINE[i], LINE[j])
    return wrap(y - dy, 4) * 4 + wrap(x - dx, 4)


def place_z(dst, chunks, z):
    n = chunks[0].shape[0]
    for k in range(8):
        dst[pl.ds(pl.multiple_of(wrap(z - RING[k], 8) * n, 8), n), :] = chunks[k][...]


def root_body(idx, *refs):
    rz, rp, mine, other, fz, fp, full = refs[:8], refs[8:12], *refs[12:]
    place_z(fz, rz, idx[0])
    n = rz[0].shape[0]
    for j in range(4):
        for i in range(4):
            fp[pl.ds(pl.multiple_of(plane_at(idx, j, i) * n, 8), n), :] = rp[j][i]
    full[...] = dot3(halves(fz[...]), halves(fp[...]), NT)
    split_rows(full, idx[3], mine, other)


def couple_body(idx, mask, *refs):
    zs, sp, mine, other, s_all, fz, full = refs[:8], refs[8:12], *refs[12:]
    core = idx[3]
    place_z(fz, zs, idx[0])
    m = sp[0].shape[2]
    for j in range(4):
        for i in range(4):
            for zz in range(4):
                at = (zz * 16 + plane_at(idx, j, i)) * m
                s_all[pl.ds(pl.multiple_of(at, 8), m), :] = sp[j][i, zz]
    full[...] = -dot3(halves(fz[...]), halves(s_all[...]), NN) * mask[...]
    h = mine.shape[0]
    first, second = full[:h, :], turn(full[h:, :])
    keep = in_half(first.shape, core)
    mine[...] = jnp.where(keep, first, second)
    other[...] = jnp.where(keep, second, first)


def factor_body(idx, wide, *refs):
    zs, out, fz = refs[:8], *refs[8:]
    cut = wide.shape[1] - fz.shape[1]
    place_z(fz, zs, idx[0])
    out[...] = dot3(halves(fz[...]), halves(wide[:, cut:]), NT)


def finish_body(idx, mine, other, deriv, owner, out):
    block = mine[...] + other[...]
    h = block.shape[0]
    out[:h, :] = block
    sums = jnp.sum(block * deriv[...], axis=0, keepdims=True)
    lane = lax.broadcasted_iota(jnp.int32, sums.shape, 1)
    row = jnp.zeros_like(sums)
    for k in range(NHYP):
        total = jnp.sum(jnp.where(owner[...] == k, sums, 0.0), axis=1, keepdims=True)
        row = jnp.where(lane == k, total, row)
    out[h:, :] = jnp.broadcast_to(row, (8, row.shape[1]))


def merge(dst, rows, zz, core):
    own = lax.div(zz, 4) == core
    m = lax.rem(zz, 4)
    keep = in_half(rows.shape, core) == own
    dst[m] = jnp.where(keep, jnp.where(own, rows, turn(rows)), dst[m])


def window(wide, at, w):
    return halves(wide[:, pl.ds(pl.multiple_of(lax.rem(at, 4) * w, 128), w)])


def subtract(full, first, second, at, panel, core):
    h = first.shape[0] - 8
    a = jnp.concatenate([first[:h, :], turn(first[:h, :])], axis=0)
    b = jnp.concatenate([second[:h, :], turn(second[:h, :])], axis=0)
    low = lax.div(at, 4) == core
    a, b = jnp.where(low, a, b), jnp.where(low, turn(b), turn(a))
    cols = jnp.where(in_half(a.shape, core), a, b)
    full[...] -= dot3(halves(cols), panel, NT)


def child_body(idx, *refs):
    cz, wide, kk, out, hi, lo = refs[:6], *refs[6:]
    z, core = idx[0], idx[3]
    w = hi.shape[1]
    hi[...], lo[...] = window(wide, z, w)
    out[...] = kk[...]
    for r in (1, 2, 3):
        first, second = cz[RING.index(r) - 1], cz[RING.index(r + 4) - 1]
        at = wrap(z - r, 8)
        subtract(out, first, second, at, window(wide, at, w), core)


def last_body(idx, *refs):
    cz, hi, lo, part, mine, other, full = refs[:8], *refs[8:]
    z, core = idx[0], idx[3]
    h = cz[0].shape[0] - 8
    n = mine.shape[1] - 8
    full[...] = part[...]
    subtract(full, cz[0], cz[7], z, (hi[...], lo[...]), core)
    total = cz[0][h:, :h]
    for k in range(1, 8):
        total += cz[k][h:, :h]
    for out, which in ((mine, core), (other, 1 - core)):
        rows = full[pl.ds(pl.multiple_of(which * h, 8), h), :].T
        for p in range(16):
            out[p, :n, :] = rows[p * n : (p + 1) * n, :]
            out[p, n:, :] = total


def own_body(idx, *refs):
    cz, out, cw = refs[:8], *refs[8:]
    z, core = idx[0], idx[3]
    n, w = cw.shape[1:]
    for k in range(8):
        rows = cz[k][pl.ds(pl.multiple_of(lax.rem(z, 4) * n, 8), n), :]
        rows = jnp.where(z >= 4, turn(rows), rows)
        merge(cw, rows, wrap(z - RING[k], 8), core)
    for m in range(4):
        out[:, m * w : (m + 1) * w] = cw[m]


def turn_blocks(a, w):
    return jnp.roll(a.reshape(a.shape[0], -1, w), w // 2, axis=2).reshape(a.shape)


def per_device(root_inv_t, child_inv_t, panel_t, deriv_t, pattern, owner):
    node, core = lax.axis_index("node"), lax.axis_index("row")
    z, y, x = node // (NY * NX), lax.rem(node // NX, NY), lax.rem(node, NX)
    plane = lax.rem(node, NY * NX)
    idx = jnp.stack([z, y, x, core]).astype(jnp.int32)
    rr, half = root_inv_t.shape
    rc, half_c = child_inv_t.shape
    sr = 2 * half
    zc = sr // NZ
    width = sr // pattern.shape[0]
    mask_all = jnp.repeat(pattern.astype(F32), width)
    owner_all = jnp.repeat(owner, width)
    mask = lax.dynamic_slice_in_dim(mask_all, core * half, half)
    mask_z = lax.dynamic_slice_in_dim(mask_all, z * zc, zc)
    keep = (lax.iota(jnp.int32, half) % zc < zc // 2) == (core == 0)
    keep_z = keep[:zc]
    owner_z = lax.dynamic_slice_in_dim(owner_all, z * zc, zc)[None, :]
    owner_z = jnp.where(keep_z[None, :], owner_z, turn_blocks(owner_z, zc))

    r_p = gather_plane(root_inv_t)
    r_z = ring_z(root_inv_t, {3: [r_p[1]]})
    panel_0, deriv_0, child_0 = lax.optimization_barrier(
        (panel_t, deriv_t, child_inv_t, r_p[0], r_z[1], r_z[2])
    )[:3]
    panel_m = panel_0 * mask[None, :]

    both = jnp.concatenate([panel_m, deriv_0], axis=0)
    both = jnp.where(keep[None, :], both, swap_core(turn_blocks(both, zc)))
    panel_k, deriv_k = both[:rc], both[rc:]
    gathered = lax.all_gather(
        jnp.concatenate([panel_k, child_0], axis=1),
        "node",
        axis=0,
        tiled=True,
        axis_index_groups=PLANES,
    )
    p_z = ring_z(panel_m, {1: [r_z[5], r_z[6]]})
    k_z = ring_z(child_0, {1: [p_z[5], p_z[6]]})

    windows = deriv_k.reshape(rc, 4, 2, zc // 2)
    own_w = jnp.where(core == 0, windows[:, :, 0], windows[:, :, 1])
    other_w = jnp.where(core == 0, windows[:, :, 1], windows[:, :, 0])
    first_w = jnp.where(core == 0, own_w, other_w)
    second_w = jnp.where(core == 0, other_w, own_w)
    send = jnp.concatenate([first_w, second_w], axis=1).transpose(1, 0, 2)
    send = after(send, r_z[7])
    d_z = exchange(send, LINES)
    d_lo = d_z[:4].reshape(4 * rc, zc // 2)
    d_hi = d_z[4:].reshape(4 * rc, zc // 2)
    d_z = jnp.where(
        core == 0, jnp.concatenate([d_lo, d_hi], axis=1), jnp.concatenate([d_hi, d_lo], axis=1)
    )

    mine, other = call(
        root_body,
        [idx, *r_z, *r_p],
        [(NZ * rr // 2, zc)] * 2,
        [pltpu.VMEM((NZ * rr, half), F32), pltpu.VMEM((16 * rr, half), F32), pltpu.VMEM((NZ * rr, zc), F32)],
        6 * NZ * rr * 16 * rr * half,
        "root_cov",
    )
    s_own = (mine + swap_core(other)).reshape(4, rr, zc)
    s_p = gather_plane(s_own)

    mine, other, s_all = call(
        couple_body,
        [idx, mask_z[None, :], *p_z, *s_p],
        [(NZ * rc // 2, zc)] * 2 + [(half, zc)],
        [pltpu.VMEM((NZ * rc, half), F32), pltpu.VMEM((NZ * rc, zc), F32)],
        6 * NZ * rc * half * zc,
        "coupling",
    )
    (c_own,) = call(
        finish_body,
        [idx, mine, swap_core(other), d_z, owner_z],
        [(4 * rc + 8, zc)],
        [],
        4 * 4 * rc * zc,
        "coupling_sum",
    )
    wide = after(gathered, c_own)

    (kk,) = call(
        factor_body,
        [idx, wide, *k_z],
        [(NZ * rc, 16 * rc)],
        [pltpu.VMEM((NZ * rc, half_c), F32)],
        6 * NZ * rc * 16 * rc * half_c,
        "factor",
    )
    root_cov = lax.dynamic_slice_in_dim(after(s_all, c_own), plane * rr, rr, axis=1).T
    c_z = ring_z(c_own, {3: [root_cov], 4: [kk]})
    part, p_hi, p_lo = call(
        child_body,
        [idx, *c_z[1:7], wide, kk],
        [(NZ * rc, 16 * rc)] + [jax.ShapeDtypeStruct((16 * rc, zc), BF16)] * 2,
        [],
        6 * 16 * rc * 3 * rc * sr,
        "child_most",
    )
    mine, other = call(
        last_body,
        [idx, *c_z, p_hi, p_lo, part],
        [(16, rc + 8, 4 * rc)] * 2,
        [pltpu.VMEM((NZ * rc, 16 * rc), F32)],
        6 * 16 * rc * rc * sr,
        "child_last",
    )

    block = mine + swap_core(other)
    got = exchange(block, PLANES)
    grad = 2.0 * jnp.sum(got[:, rc, :NHYP], axis=0)
    got = got[:, :rc]

    late = lax.optimization_barrier((*c_z, block))
    (c_rows,) = call(
        own_body, [idx, *late[:8]], [(rc, half)], [pltpu.VMEM((4, rc, zc), F32)], 4 * rc * half, "own_rows"
    )
    coupling = jnp.where(keep[None, :], c_rows, turn_blocks(swap_core(c_rows), zc))
    child_cov = got.reshape(16, rc, 4, rc).transpose(1, 2, 0, 3).reshape(rc, half_c)
    return (root_cov, coupling, child_cov, grad)


def solution(mesh):
    placed = (P("node", "row"), P("node", "row"), P("node", "row"), P("node", "row"), P(), P())
    return jax.shard_map(
        per_device,
        mesh=mesh,
        in_specs=placed,
        out_specs=(P("node", "row"), P("node", "row"), P("node", "row"), P()),
        check_vma=False,
    )
```

```python
import functools

import jax
import jax.numpy as jnp
from jax import lax
from jax.experimental import pallas as pl
from jax.experimental.pallas import tpu as pltpu
from jax.sharding import PartitionSpec as P

NHYP = 4
NZ, NY, NX = 8, 4, 4
NODES = [(z, y, x) for z in range(NZ) for y in range(NY) for x in range(NX)]
PLANES = [[z * NY * NX + i for i in range(NY * NX)] for z in range(NZ)]
VMEM = pl.BlockSpec(memory_space=pltpu.VMEM)
ANY = pl.BlockSpec(memory_space=pl.ANY)
SMEM = pl.BlockSpec(memory_space=pltpu.SMEM)
F32, BF16 = jnp.float32, jnp.bfloat16


def node_id(z, y, x):
    return ((z % NZ) * NY + y % NY) * NX + x % NX


def shift(a, dz=0, dy=0, dx=0):
    perm = [(node_id(z, y, x), node_id(z + dz, y + dy, x + dx)) for z, y, x in NODES]
    return lax.ppermute(a, "node", perm)


def shift_cores(a, first, second):
    perm = []
    for z, y, x in NODES:
        for core, (dz, dy, dx) in enumerate((first, second)):
            perm.append((node_id(z, y, x) * 2 + core, node_id(z + dz, y + dy, x + dx) * 2 + core))
    return lax.ppermute(a, ("node", "row"), perm)


def swap_core(a):
    return lax.ppermute(a, "row", [(0, 1), (1, 0)])


RING = (0, 1, 7, 2, 6, 3, 5, 4)
LINE = (0, 1, 3, 2)


def after(a, *others):
    return lax.optimization_barrier((a, *others))[0]


def ring_steps(a):
    up, down = a, a
    chunks = [a]
    for k in range(1, 5):
        late = yield chunks
        up, down = lax.optimization_barrier((up, down, *late))[:2]
        if k < 4:
            up = shift(up, dz=1)
            down = shift(down, dz=-1)
            chunks = chunks + [up, down]
        else:
            last = jnp.where(lax.axis_index("row") == 0, up, down)
            chunks = chunks + [shift_cores(last, (1, 0, 0), (-1, 0, 0))]
    yield chunks


def ring_z(a, late=()):
    late = dict(late)
    steps = ring_steps(a)
    chunks = next(steps)
    for k in range(1, 5):
        chunks = steps.send(late.get(k, ()))
    return chunks


def plane_first(a):
    return jnp.stack([a] + [shift_cores(a, (0, 0, k), (0, k, 0)) for k in LINE[1:]])


def plane_second(a):
    return [a] + [shift_cores(a, (0, k, 0), (0, 0, k)) for k in LINE[1:]]


LINES = [[z * NY * NX + i for z in range(NZ)] for i in range(NY * NX)]


def exchange(blocks, groups):
    return lax.all_to_all(blocks, "node", 0, 0, axis_index_groups=groups, tiled=True)


def halves(x):
    hi = x.astype(BF16)
    return hi, (x - hi.astype(F32)).astype(BF16)


def dot3(a, b, dims):
    d = functools.partial(
        lax.dot_general, dimension_numbers=(dims, ((), ())), preferred_element_type=F32
    )
    return d(a[0], b[0]) + (d(a[0], b[1]) + d(a[1], b[0]))


NT, NN = ((1,), (1,)), ((1,), (0,))


def call(body, idx, far, near, outs, scratch, copies, flops, name, limit=None):
    outs = [o if hasattr(o, "dtype") else jax.ShapeDtypeStruct(o, F32) for o in outs]
    vmem = sum(a.size * a.dtype.itemsize for a in [*near, *outs])
    vmem += sum(s.dtype.itemsize * functools.reduce(lambda p, q: p * q, s.shape) for s in scratch)
    moved = vmem + sum(a.size * a.dtype.itemsize for a in far)
    return pl.pallas_call(
        body,
        out_shape=outs,
        in_specs=[SMEM] + [ANY] * len(far) + [VMEM] * len(near),
        out_specs=[VMEM] * len(outs),
        scratch_shapes=[*scratch] + [pltpu.SemaphoreType.DMA((copies,))] * (copies > 0),
        cost_estimate=pl.CostEstimate(flops=flops, bytes_accessed=moved // 2, transcendentals=0),
        compiler_params=pltpu.CompilerParams(vmem_limit_bytes=limit or min(56 << 20, 2 * vmem + (8 << 20))),
        name=name,
    )(idx, *far, *near)


def fetch(sems, pairs, first=0):
    copies = [pltpu.make_async_copy(a, b, sems.at[first + i]) for i, (a, b) in enumerate(pairs)]
    for copy in copies:
        copy.start()
    return copies


def wait(copies):
    for copy in copies:
        copy.wait()


def wrap(v, n):
    return lax.rem(v + n, n)


def split_rows(full, core, mine, other):
    h = mine.shape[0]
    mine[...] = full[pl.ds(pl.multiple_of(core * h, 8), h), :]
    other[...] = full[pl.ds(pl.multiple_of((1 - core) * h, 8), h), :]


def turn(a):
    return pltpu.roll(a, a.shape[-1] // 2, axis=a.ndim - 1)


def in_half(shape, core):
    return (lax.broadcasted_iota(jnp.int32, shape, len(shape) - 1) < shape[-1] // 2) == (core == 0)


def plane_at(idx, j, i):
    y, x, core = idx[1], idx[2], idx[3]
    dy = jnp.where(core == 0, LINE[j], LINE[i])
    dx = jnp.where(core == 0, LINE[i], LINE[j])
    return wrap(y - dy, 4) * 4 + wrap(x - dx, 4)


def rows_at(dst, row, n):
    return dst.at[pl.ds(pl.multiple_of(row, 8), n), :]


def line_pairs(chunks, dst, z, first=0):
    n = dst.shape[0] // NZ
    return [
        (chunks[k].at[first : first + n, :], rows_at(dst, wrap(z - RING[k], 8) * n, n)) for k in range(8)
    ]


def turn_cols(a, w):
    return jnp.concatenate(
        [turn(a[:, m * w : (m + 1) * w]) for m in range(a.shape[1] // w)], axis=1
    )


def give_body(idx, panel, deriv, mask, out):
    n, w = panel.shape[0], mask.shape[1] // 4
    out[:n, :] = turn_cols(panel[...] * mask[...], w)
    out[n:, :] = turn_cols(deriv[...], w)


def take_body(idx, panel, deriv, mask, child, got, wide, first, second):
    n, half = panel.shape
    w = half // 4
    core = idx[3]
    masked = panel[...] * mask[...]
    wide[:, half:] = child[...]
    for m in range(4):
        cols = slice(m * w, (m + 1) * w)
        keep = in_half((n, w), core)
        wide[:, cols] = jnp.where(keep, masked[:, cols], got[:n, cols])
        moved = jnp.where(keep, deriv[:, cols], got[n:, cols])
        swapped = turn(moved)
        first[m] = moved[:, : w // 2]
        second[m] = swapped[:, : w // 2]


def root_body(idx, *refs):
    rz, rp, mine, other, fz, fp, full, sems = refs[:8], refs[8:12], *refs[12:]
    n = fz.shape[0] // NZ
    pairs = line_pairs(rz, fz, idx[0])
    for j in range(4):
        for i in range(4):
            pairs.append((rp[j].at[i], rows_at(fp, plane_at(idx, j, i) * n, n)))
    wait(fetch(sems, pairs))
    full[...] = dot3(halves(fz[...]), halves(fp[...]), NT)
    split_rows(full, idx[3], mine, other)


def couple_body(idx, *refs):
    zs, sp, mask, mask_z, mine, other, s_all, fz, full, sems = refs[:8], refs[8:12], *refs[12:]
    core = idx[3]
    pairs = line_pairs(zs, fz, idx[0], sp[0].shape[2])
    for j in range(4):
        for i in range(4):
            pairs.append((sp[j].at[i], s_all.at[:, plane_at(idx, j, i)]))
    wait(fetch(sems, pairs))
    s_cols = s_all[...].reshape(fz.shape[1], full.shape[1])
    full[...] = -dot3(halves(fz[...] * mask[...]), halves(s_cols), NN) * mask_z[...]
    h = mine.shape[0]
    first, second = full[:h, :], turn(full[h:, :])
    keep = in_half(first.shape, core)
    mine[...] = jnp.where(keep, first, second)
    other[...] = jnp.where(keep, second, first)


def factor_body(half, idx, *refs):
    zs, wide, add, out, fz, fp, sems = refs[:8], refs[8], refs[9:-4], *refs[-4:]
    n, w = zs[0].shape
    part = w // 2
    cols = slice(half * part, (half + 1) * part)
    cut = wide.shape[1] - w + half * part
    pairs = [(wide.at[:, cut : cut + part], fp)]
    for k in range(8):
        pairs.append((zs[k].at[:, cols], rows_at(fz, wrap(idx[0] - RING[k], 8) * n, n)))
    wait(fetch(sems, pairs))
    term = dot3(halves(fz[...]), halves(fp[...]), NT)
    out[...] = add[0][...] + term if add else term


def finish_body(idx, got, mine, deriv, owner, out):
    block = mine[...] + got[...]
    h = block.shape[0]
    out[:h, :] = block
    sums = jnp.sum(block * deriv[...], axis=0, keepdims=True)
    lane = lax.broadcasted_iota(jnp.int32, sums.shape, 1)
    row = jnp.zeros_like(sums)
    for k in range(NHYP):
        total = jnp.sum(jnp.where(owner[...] == k, sums, 0.0), axis=1, keepdims=True)
        row = jnp.where(lane == k, total, row)
    out[h:, :] = jnp.broadcast_to(row, (8, row.shape[1]))


def merge(dst, rows, zz, core):
    own = lax.div(zz, 4) == core
    m = lax.rem(zz, 4)
    keep = in_half(rows.shape, core) == own
    dst[m] = jnp.where(keep, jnp.where(own, rows, turn(rows)), dst[m])


def window(panel, at, w):
    return halves(panel[:, pl.ds(pl.multiple_of(lax.rem(at, 4) * w, 128), w)])


def subtract(full, first, second, at, panel, core):
    h = first.shape[0] - 8
    a = jnp.concatenate([first[:h, :], turn(first[:h, :])], axis=0)
    b = jnp.concatenate([second[:h, :], turn(second[:h, :])], axis=0)
    low = lax.div(at, 4) == core
    a, b = jnp.where(low, a, b), jnp.where(low, turn(b), turn(a))
    cols = jnp.where(in_half(a.shape, core), a, b)
    full[...] -= dot3(halves(cols), panel, NT)


def child_body(idx, *refs):
    cz, wide, kk, out, hi, lo = refs[:6], *refs[6:]
    z, core = idx[0], idx[3]
    w = hi.shape[1]
    out[...] = kk[...]
    for r in (1, 2, 3):
        first, second = cz[RING.index(r) - 1], cz[RING.index(r + 4) - 1]
        at = wrap(z - r, 8)
        subtract(out, first, second, at, window(wide, at, w), core)
    hi[...], lo[...] = window(wide, z, w)


def last_body(idx, *refs):
    cz, hi, lo, part, mine, other, own, full, cw = refs[:8], *refs[8:]
    z, core = idx[0], idx[3]
    h = cz[0].shape[0] - 8
    n = mine.shape[1] - 8
    w = cw.shape[2]
    full[...] = part[...]
    subtract(full, cz[0], cz[7], z, (hi[...], lo[...]), core)
    total = cz[0][h:, :h]
    for k in range(1, 8):
        total += cz[k][h:, :h]
    for out, which in ((mine, core), (other, 1 - core)):
        rows = full[pl.ds(pl.multiple_of(which * h, 8), h), :].T
        for p in range(16):
            out[p, :n, :] = rows[p * n : (p + 1) * n, :]
            out[p, n:, :] = total
    at = pl.multiple_of(lax.rem(z, 4) * n, 8)
    for k in range(8):
        rows = cz[k][pl.ds(at, n), :]
        rows = jnp.where(z >= 4, turn(rows), rows)
        merge(cw, rows, wrap(z - RING[k], 8), core)
    for m in range(4):
        own[:, m * w : (m + 1) * w] = cw[m]


def turn_blocks(a, w):
    return jnp.roll(a.reshape(a.shape[0], -1, w), w // 2, axis=2).reshape(a.shape)


def per_device(root_inv_t, child_inv_t, panel_t, deriv_t, pattern, owner):
    node, core = lax.axis_index("node"), lax.axis_index("row")
    z, y, x = node // (NY * NX), lax.rem(node // NX, NY), lax.rem(node, NX)
    plane = lax.rem(node, NY * NX)
    idx = jnp.stack([z, y, x, core]).astype(jnp.int32)
    rr, half = root_inv_t.shape
    rc, half_c = child_inv_t.shape
    sr = 2 * half
    zc = sr // NZ
    width = sr // pattern.shape[0]
    mask_all = jnp.repeat(pattern.astype(F32), width)
    owner_all = jnp.repeat(owner, width)
    mask = lax.dynamic_slice_in_dim(mask_all, core * half, half)
    mask_z = lax.dynamic_slice_in_dim(mask_all, z * zc, zc)
    keep = (lax.iota(jnp.int32, half) % zc < zc // 2) == (core == 0)
    keep_z = keep[:zc]
    owner_z = lax.dynamic_slice_in_dim(owner_all, z * zc, zc)[None, :]
    owner_z = jnp.where(keep_z[None, :], owner_z, turn_blocks(owner_z, zc))

    mask_row = mask[None, :]
    r_first = plane_first(root_inv_t)
    r_p = plane_second(r_first)
    r_z = ring_z(jnp.concatenate([root_inv_t, panel_t], axis=0), {2: [r_first], 3: r_p[1:3], 4: [r_p[3]]})
    (given,) = call(
        give_body, idx, [], [panel_t, deriv_t, mask_row], [(2 * rc, half)], [], 0, 2 * rc * half, "give"
    )
    wide_own, first_w, second_w = call(
        take_body,
        idx,
        [],
        [panel_t, deriv_t, mask_row, child_inv_t, swap_core(given)],
        [(rc, half + half_c)] + [(4, rc, zc // 2)] * 2,
        [],
        0,
        4 * rc * half,
        "take",
    )
    gathered = lax.all_gather(wide_own, "node", axis=0, tiled=True, axis_index_groups=PLANES)
    steps = ring_steps(child_inv_t)
    next(steps)
    k_1 = steps.send([r_z[7]])

    send = jnp.concatenate([first_w, second_w], axis=0)
    send = after(send, r_z[7])
    d_z = exchange(send, LINES)
    d_lo = d_z[:4].reshape(4 * rc, zc // 2)
    d_hi = d_z[4:].reshape(4 * rc, zc // 2)
    d_z = jnp.where(
        core == 0, jnp.concatenate([d_lo, d_hi], axis=1), jnp.concatenate([d_hi, d_lo], axis=1)
    )

    mine, other = call(
        root_body,
        idx,
        [*r_z, *r_p],
        [],
        [(NZ * rr // 2, zc)] * 2,
        [pltpu.VMEM((NZ * rr, half), F32), pltpu.VMEM((16 * rr, half), F32), pltpu.VMEM((NZ * rr, zc), F32)],
        24,
        6 * NZ * rr * 16 * rr * half,
        "root_cov",
        60 << 20,
    )
    s_own = (mine + swap_core(other)).reshape(4, rr, zc)
    s_first = plane_first(s_own)
    s_first = after(s_first, k_1[1], k_1[2])
    s_p = plane_second(s_first)
    k_2 = steps.send([])
    s_p[1] = after(s_p[1], k_2[3], k_2[4])

    mine, other, s_all = call(
        couple_body,
        idx,
        [*r_z, *s_p],
        [mask_row, mask_z[None, :]],
        [(NZ * rc // 2, zc)] * 2 + [(4, 16, rr, zc)],
        [pltpu.VMEM((NZ * rc, half), F32), pltpu.VMEM((NZ * rc, zc), F32)],
        24,
        6 * NZ * rc * half * zc,
        "coupling",
        60 << 20,
    )
    (c_own,) = call(
        finish_body,
        idx,
        [],
        [swap_core(other), mine, d_z, owner_z],
        [(4 * rc + 8, zc)],
        [],
        0,
        4 * 4 * rc * zc,
        "coupling_sum",
    )
    k_3 = steps.send([])
    c_own = after(c_own, k_3[5], k_3[6])
    k_z = steps.send([])
    wide = after(gathered, c_own)

    kk = []
    for part in range(2):
        kk = call(
            functools.partial(factor_body, part),
            idx,
            [*k_z, wide],
            kk,
            [(NZ * rc, 16 * rc)],
            [pltpu.VMEM((NZ * rc, half_c // 2), F32), pltpu.VMEM((16 * rc, half_c // 2), F32)],
            9,
            3 * NZ * rc * 16 * rc * half_c,
            "factor",
            60 << 20,
        )
        if part == 0:
            (kk_first,) = kk
    (kk,) = kk
    root_cov = after(s_all, c_own).reshape(half, zc)
    root_cov = lax.dynamic_slice_in_dim(root_cov, plane * rr, rr, axis=1).T
    c_z = ring_z(c_own, {2: [root_cov], 3: [kk_first], 4: [kk]})
    part, p_hi, p_lo = call(
        child_body,
        idx,
        [],
        [*c_z[1:7], wide, kk],
        [(NZ * rc, 16 * rc)] + [jax.ShapeDtypeStruct((16 * rc, zc), BF16)] * 2,
        [],
        0,
        6 * 16 * rc * 3 * rc * sr,
        "child_most",
    )
    mine, other, c_rows = call(
        last_body,
        idx,
        [],
        [*c_z, p_hi, p_lo, part],
        [(16, rc + 8, 4 * rc)] * 2 + [(rc, half)],
        [pltpu.VMEM((NZ * rc, 16 * rc), F32), pltpu.VMEM((4, rc, zc), F32)],
        0,
        6 * 16 * rc * rc * sr,
        "child_last",
    )

    block = mine + swap_core(other)
    got = exchange(block, PLANES)
    grad = 2.0 * jnp.sum(got[:, rc, :NHYP], axis=0)
    got = got[:, :rc]

    coupling = jnp.where(keep[None, :], c_rows, turn_blocks(swap_core(c_rows), zc))
    child_cov = got.reshape(16, rc, 4, rc).transpose(1, 2, 0, 3).reshape(rc, half_c)
    return (root_cov, coupling, child_cov, grad)


def solution(mesh):
    placed = (P("node", "row"), P("node", "row"), P("node", "row"), P("node", "row"), P(), P())
    return jax.shard_map(
        per_device,
        mesh=mesh,
        in_specs=placed,
        out_specs=(P("node", "row"), P("node", "row"), P("node", "row"), P()),
        check_vma=False,
    )
```

```python
import functools

import jax
import jax.numpy as jnp
from jax import lax
from jax.experimental import pallas as pl
from jax.experimental.pallas import tpu as pltpu
from jax.sharding import PartitionSpec as P

NHYP = 4
NZ, NY, NX = 8, 4, 4
NODES = [(z, y, x) for z in range(NZ) for y in range(NY) for x in range(NX)]
PLANES = [[z * NY * NX + i for i in range(NY * NX)] for z in range(NZ)]
VMEM = pl.BlockSpec(memory_space=pltpu.VMEM)
ANY = pl.BlockSpec(memory_space=pl.ANY)
SMEM = pl.BlockSpec(memory_space=pltpu.SMEM)
F32, BF16 = jnp.float32, jnp.bfloat16


def node_id(z, y, x):
    return ((z % NZ) * NY + y % NY) * NX + x % NX


def shift(a, dz=0, dy=0, dx=0):
    perm = [(node_id(z, y, x), node_id(z + dz, y + dy, x + dx)) for z, y, x in NODES]
    return lax.ppermute(a, "node", perm)


def shift_cores(a, first, second):
    perm = []
    for z, y, x in NODES:
        for core, (dz, dy, dx) in enumerate((first, second)):
            perm.append((node_id(z, y, x) * 2 + core, node_id(z + dz, y + dy, x + dx) * 2 + core))
    return lax.ppermute(a, ("node", "row"), perm)


def swap_core(a):
    return lax.ppermute(a, "row", [(0, 1), (1, 0)])


RING = (0, 1, 7, 2, 6, 3, 5, 4)
LINE = (0, 1, 3, 2)


def after(a, *others):
    return lax.optimization_barrier((a, *others))[0]


def ring_steps(a):
    up, down = a, a
    chunks = [a]
    for k in range(1, 5):
        late = yield chunks
        up, down = lax.optimization_barrier((up, down, *late))[:2]
        if k < 4:
            up = shift(up, dz=1)
            down = shift(down, dz=-1)
            chunks = chunks + [up, down]
        else:
            last = jnp.where(lax.axis_index("row") == 0, up, down)
            chunks = chunks + [shift_cores(last, (1, 0, 0), (-1, 0, 0))]
    yield chunks


def ring_z(a, late=()):
    late = dict(late)
    steps = ring_steps(a)
    chunks = next(steps)
    for k in range(1, 5):
        chunks = steps.send(late.get(k, ()))
    return chunks


def plane_first(a):
    return jnp.stack([a] + [shift_cores(a, (0, 0, k), (0, k, 0)) for k in LINE[1:]])


def plane_second(a):
    return [a] + [shift_cores(a, (0, k, 0), (0, 0, k)) for k in LINE[1:]]


LINES = [[z * NY * NX + i for z in range(NZ)] for i in range(NY * NX)]


def exchange(blocks, groups):
    return lax.all_to_all(blocks, "node", 0, 0, axis_index_groups=groups, tiled=True)


def halves(x):
    hi = x.astype(BF16)
    return hi, (x - hi.astype(F32)).astype(BF16)


def dot3(a, b, dims):
    d = functools.partial(
        lax.dot_general, dimension_numbers=(dims, ((), ())), preferred_element_type=F32
    )
    return d(a[0], b[0]) + (d(a[0], b[1]) + d(a[1], b[0]))


NT, NN = ((1,), (1,)), ((1,), (0,))


def call(body, idx, far, near, outs, scratch, copies, flops, name, limit=None):
    outs = [o if hasattr(o, "dtype") else jax.ShapeDtypeStruct(o, F32) for o in outs]
    vmem = sum(a.size * a.dtype.itemsize for a in [*near, *outs])
    vmem += sum(s.dtype.itemsize * functools.reduce(lambda p, q: p * q, s.shape) for s in scratch)
    moved = vmem + sum(a.size * a.dtype.itemsize for a in far)
    return pl.pallas_call(
        body,
        out_shape=outs,
        in_specs=[SMEM] + [ANY] * len(far) + [VMEM] * len(near),
        out_specs=[VMEM] * len(outs),
        scratch_shapes=[*scratch] + [pltpu.SemaphoreType.DMA((copies,))] * (copies > 0),
        cost_estimate=pl.CostEstimate(flops=flops, bytes_accessed=moved // 2, transcendentals=0),
        compiler_params=pltpu.CompilerParams(vmem_limit_bytes=limit or min(56 << 20, 2 * vmem + (8 << 20))),
        name=name,
    )(idx, *far, *near)


def fetch(sems, pairs, first=0):
    copies = [pltpu.make_async_copy(a, b, sems.at[first + i]) for i, (a, b) in enumerate(pairs)]
    for copy in copies:
        copy.start()
    return copies


def wait(copies):
    for copy in copies:
        copy.wait()


def wrap(v, n):
    return lax.rem(v + n, n)


def split_rows(full, core, mine, other):
    h = mine.shape[0]
    mine[...] = full[pl.ds(pl.multiple_of(core * h, 8), h), :]
    other[...] = full[pl.ds(pl.multiple_of((1 - core) * h, 8), h), :]


def turn(a):
    return pltpu.roll(a, a.shape[-1] // 2, axis=a.ndim - 1)


def in_half(shape, core):
    return (lax.broadcasted_iota(jnp.int32, shape, len(shape) - 1) < shape[-1] // 2) == (core == 0)


def plane_at(idx, j, i):
    y, x, core = idx[1], idx[2], idx[3]
    dy = jnp.where(core == 0, LINE[j], LINE[i])
    dx = jnp.where(core == 0, LINE[i], LINE[j])
    return wrap(y - dy, 4) * 4 + wrap(x - dx, 4)


def rows_at(dst, row, n):
    return dst.at[pl.ds(pl.multiple_of(row, 8), n), :]


def line_pairs(chunks, dst, z, first=0):
    n = dst.shape[0] // NZ
    return [
        (chunks[k].at[first : first + n, :], rows_at(dst, wrap(z - RING[k], 8) * n, n)) for k in range(8)
    ]


def take_body(idx, panel, child, got, mask, wide):
    n, half = panel.shape
    w = half // 4
    keep = in_half((n, w), idx[3])
    for m in range(4):
        cols = slice(m * w, (m + 1) * w)
        wide[:, cols] = jnp.where(keep, panel[:, cols], turn(got[:, cols])) * mask[:, cols]
    wide[:, half:] = child[...]


def take_deriv_body(idx, deriv, got, first, second):
    n, half = deriv.shape
    w = half // 4
    keep = in_half((n, w), idx[3])
    for m in range(4):
        cols = slice(m * w, (m + 1) * w)
        moved = jnp.where(keep, deriv[:, cols], turn(got[:, cols]))
        first[m] = moved[:, : w // 2]
        second[m] = turn(moved)[:, : w // 2]


def root_body(idx, *refs):
    rz, rp, mine, other, fz, fp, full, sems = refs[:8], refs[8:12], *refs[12:]
    n = fz.shape[0] // NZ
    pairs = line_pairs(rz, fz, idx[0])
    for j in range(4):
        for i in range(4):
            pairs.append((rp[j].at[i], rows_at(fp, plane_at(idx, j, i) * n, n)))
    wait(fetch(sems, pairs))
    full[...] = dot3(halves(fz[...]), halves(fp[...]), NT)
    split_rows(full, idx[3], mine, other)


def couple_body(idx, *refs):
    zs, sp, mask, mask_z, mine, other, s_all, fz, full, sems = refs[:8], refs[8:12], *refs[12:]
    core = idx[3]
    early = fetch(sems, line_pairs(zs, fz, idx[0], sp[0].shape[2]))
    pairs = []
    for j in range(4):
        for i in range(4):
            pairs.append((sp[j].at[i], s_all.at[:, plane_at(idx, j, i)]))
    late = fetch(sems, pairs, 8)
    wait(early)
    panel = halves(fz[...] * mask[...])
    wait(late)
    s_cols = s_all[...].reshape(fz.shape[1], full.shape[1])
    full[...] = -dot3(panel, halves(s_cols), NN) * mask_z[...]
    h = mine.shape[0]
    first, second = full[:h, :], turn(full[h:, :])
    keep = in_half(first.shape, core)
    mine[...] = jnp.where(keep, first, second)
    other[...] = jnp.where(keep, second, first)


def factor_body(half, idx, *refs):
    zs, wide, add, out, fz, fp, sems = refs[:8], refs[8], refs[9:-4], *refs[-4:]
    n, w = zs[0].shape
    part = w // 2
    cols = slice(half * part, (half + 1) * part)
    cut = wide.shape[1] - w + half * part
    pairs = [(wide.at[:, cut : cut + part], fp)]
    for k in range(8):
        pairs.append((zs[k].at[:, cols], rows_at(fz, wrap(idx[0] - RING[k], 8) * n, n)))
    wait(fetch(sems, pairs))
    term = dot3(halves(fz[...]), halves(fp[...]), NT)
    out[...] = add[0][...] + term if add else term


def finish_body(idx, got, mine, deriv, owner, out):
    block = mine[...] + got[...]
    h = block.shape[0]
    out[:h, :] = block
    sums = jnp.sum(block * deriv[...], axis=0, keepdims=True)
    lane = lax.broadcasted_iota(jnp.int32, sums.shape, 1)
    row = jnp.zeros_like(sums)
    for k in range(NHYP):
        total = jnp.sum(jnp.where(owner[...] == k, sums, 0.0), axis=1, keepdims=True)
        row = jnp.where(lane == k, total, row)
    out[h:, :] = jnp.broadcast_to(row, (8, row.shape[1]))


def merge(dst, rows, zz, core):
    own = lax.div(zz, 4) == core
    m = lax.rem(zz, 4)
    keep = in_half(rows.shape, core) == own
    dst[m] = jnp.where(keep, jnp.where(own, rows, turn(rows)), dst[m])


def window(panel, at, w):
    return halves(panel[:, pl.ds(pl.multiple_of(lax.rem(at, 4) * w, 128), w)])


def subtract(full, first, second, at, panel, core):
    h = first.shape[0] - 8
    a = jnp.concatenate([first[:h, :], turn(first[:h, :])], axis=0)
    b = jnp.concatenate([second[:h, :], turn(second[:h, :])], axis=0)
    low = lax.div(at, 4) == core
    a, b = jnp.where(low, a, b), jnp.where(low, turn(b), turn(a))
    cols = jnp.where(in_half(a.shape, core), a, b)
    full[...] -= dot3(halves(cols), panel, NT)


def child_body(idx, *refs):
    cz, wide, kk, out, hi, lo = refs[:6], *refs[6:]
    z, core = idx[0], idx[3]
    w = hi.shape[1]
    out[...] = kk[...]
    for r in (1, 2, 3):
        first, second = cz[RING.index(r) - 1], cz[RING.index(r + 4) - 1]
        at = wrap(z - r, 8)
        subtract(out, first, second, at, window(wide, at, w), core)
    hi[...], lo[...] = window(wide, z, w)


def last_body(idx, *refs):
    cz, hi, lo, part, mine, other, own, full, cw = refs[:8], *refs[8:]
    z, core = idx[0], idx[3]
    h = cz[0].shape[0] - 8
    n = mine.shape[1] - 8
    w = cw.shape[2]
    full[...] = part[...]
    subtract(full, cz[0], cz[7], z, (hi[...], lo[...]), core)
    total = cz[0][h:, :h]
    for k in range(1, 8):
        total += cz[k][h:, :h]
    for out, which in ((mine, core), (other, 1 - core)):
        rows = full[pl.ds(pl.multiple_of(which * h, 8), h), :].T
        for p in range(16):
            out[p, :n, :] = rows[p * n : (p + 1) * n, :]
            out[p, n:, :] = total
    at = pl.multiple_of(lax.rem(z, 4) * n, 8)
    for k in range(8):
        rows = cz[k][pl.ds(at, n), :]
        rows = jnp.where(z >= 4, turn(rows), rows)
        merge(cw, rows, wrap(z - RING[k], 8), core)
    for m in range(4):
        own[:, m * w : (m + 1) * w] = cw[m]


def turn_blocks(a, w):
    return jnp.roll(a.reshape(a.shape[0], -1, w), w // 2, axis=2).reshape(a.shape)


def per_device(root_inv_t, child_inv_t, panel_t, deriv_t, pattern, owner):
    node, core = lax.axis_index("node"), lax.axis_index("row")
    z, y, x = node // (NY * NX), lax.rem(node // NX, NY), lax.rem(node, NX)
    plane = lax.rem(node, NY * NX)
    idx = jnp.stack([z, y, x, core]).astype(jnp.int32)
    rr, half = root_inv_t.shape
    rc, half_c = child_inv_t.shape
    sr = 2 * half
    zc = sr // NZ
    width = sr // pattern.shape[0]
    mask_all = jnp.repeat(pattern.astype(F32), width)
    owner_all = jnp.repeat(owner, width)
    mask = lax.dynamic_slice_in_dim(mask_all, core * half, half)
    mask_z = lax.dynamic_slice_in_dim(mask_all, z * zc, zc)
    keep = (lax.iota(jnp.int32, half) % zc < zc // 2) == (core == 0)
    keep_z = keep[:zc]
    owner_z = lax.dynamic_slice_in_dim(owner_all, z * zc, zc)[None, :]
    owner_z = jnp.where(keep_z[None, :], owner_z, turn_blocks(owner_z, zc))

    mask_row = mask[None, :]
    r_first = plane_first(root_inv_t)
    r_p = plane_second(r_first)
    r_z = ring_z(jnp.concatenate([root_inv_t, panel_t], axis=0), {2: [r_first], 3: r_p[1:3], 4: [r_p[3]]})
    mask_other = lax.dynamic_slice_in_dim(mask_all, (1 - core) * half, half)[None, :]
    mask_k = jnp.where(keep[None, :], mask_row, turn_blocks(mask_other, zc))
    (wide_own,) = call(
        take_body,
        idx,
        [],
        [panel_t, child_inv_t, swap_core(panel_t), mask_k],
        [(rc, half + half_c)],
        [],
        0,
        2 * rc * half,
        "take",
    )
    gathered = lax.all_gather(wide_own, "node", axis=0, tiled=True, axis_index_groups=PLANES)
    steps = ring_steps(child_inv_t)
    next(steps)
    k_1 = steps.send([r_z[7]])

    deriv_0 = after(deriv_t, r_z[3], r_z[4])
    first_w, second_w = call(
        take_deriv_body,
        idx,
        [],
        [deriv_0, swap_core(deriv_0)],
        [(4, rc, zc // 2)] * 2,
        [],
        0,
        2 * rc * half,
        "take_deriv",
    )
    send = jnp.concatenate([first_w, second_w], axis=0)
    send = after(send, r_z[7])
    d_z = exchange(send, LINES)
    d_lo = d_z[:4].reshape(4 * rc, zc // 2)
    d_hi = d_z[4:].reshape(4 * rc, zc // 2)
    d_z = jnp.where(
        core == 0, jnp.concatenate([d_lo, d_hi], axis=1), jnp.concatenate([d_hi, d_lo], axis=1)
    )

    mine, other = call(
        root_body,
        idx,
        [*r_z, *r_p],
        [],
        [(NZ * rr // 2, zc)] * 2,
        [pltpu.VMEM((NZ * rr, half), F32), pltpu.VMEM((16 * rr, half), F32), pltpu.VMEM((NZ * rr, zc), F32)],
        24,
        6 * NZ * rr * 16 * rr * half,
        "root_cov",
        60 << 20,
    )
    s_own = (mine + swap_core(other)).reshape(4, rr, zc)
    s_first = plane_first(s_own)
    s_first = after(s_first, k_1[1], k_1[2])
    s_p = plane_second(s_first)
    k_2 = steps.send([])
    s_p[1] = after(s_p[1], k_2[3], k_2[4])

    mine, other, s_all = call(
        couple_body,
        idx,
        [*r_z, *s_p],
        [mask_row, mask_z[None, :]],
        [(NZ * rc // 2, zc)] * 2 + [(4, 16, rr, zc)],
        [pltpu.VMEM((NZ * rc, half), F32), pltpu.VMEM((NZ * rc, zc), F32)],
        24,
        6 * NZ * rc * half * zc,
        "coupling",
        60 << 20,
    )
    (c_own,) = call(
        finish_body,
        idx,
        [],
        [swap_core(other), mine, d_z, owner_z],
        [(4 * rc + 8, zc)],
        [],
        0,
        4 * 4 * rc * zc,
        "coupling_sum",
    )
    k_3 = steps.send([])
    c_own = after(c_own, k_3[5], k_3[6])
    k_z = steps.send([])
    wide = after(gathered, c_own)

    kk = []
    for part in range(2):
        kk = call(
            functools.partial(factor_body, part),
            idx,
            [*k_z, wide],
            kk,
            [(NZ * rc, 16 * rc)],
            [pltpu.VMEM((NZ * rc, half_c // 2), F32), pltpu.VMEM((16 * rc, half_c // 2), F32)],
            9,
            3 * NZ * rc * 16 * rc * half_c,
            "factor",
            60 << 20,
        )
        if part == 0:
            (kk_first,) = kk
    (kk,) = kk
    root_cov = after(s_all, c_own).reshape(half, zc)
    root_cov = lax.dynamic_slice_in_dim(root_cov, plane * rr, rr, axis=1).T
    c_z = ring_z(c_own, {2: [root_cov], 3: [kk_first], 4: [kk]})
    part, p_hi, p_lo = call(
        child_body,
        idx,
        [],
        [*c_z[1:7], wide, kk],
        [(NZ * rc, 16 * rc)] + [jax.ShapeDtypeStruct((16 * rc, zc), BF16)] * 2,
        [],
        0,
        6 * 16 * rc * 3 * rc * sr,
        "child_most",
    )
    mine, other, c_rows = call(
        last_body,
        idx,
        [],
        [*c_z, p_hi, p_lo, part],
        [(16, rc + 8, 4 * rc)] * 2 + [(rc, half)],
        [pltpu.VMEM((NZ * rc, 16 * rc), F32), pltpu.VMEM((4, rc, zc), F32)],
        0,
        6 * 16 * rc * rc * sr,
        "child_last",
    )

    block = mine + swap_core(other)
    got = exchange(block, PLANES)
    grad = 2.0 * jnp.sum(got[:, rc, :NHYP], axis=0)
    got = got[:, :rc]

    coupling = jnp.where(keep[None, :], c_rows, turn_blocks(swap_core(c_rows), zc))
    child_cov = got.reshape(16, rc, 4, rc).transpose(1, 2, 0, 3).reshape(rc, half_c)
    return (root_cov, coupling, child_cov, grad)


def solution(mesh):
    placed = (P("node", "row"), P("node", "row"), P("node", "row"), P("node", "row"), P(), P())
    return jax.shard_map(
        per_device,
        mesh=mesh,
        in_specs=placed,
        out_specs=(P("node", "row"), P("node", "row"), P("node", "row"), P()),
        check_vma=False,
    )
```

```python
import functools

import jax
import jax.numpy as jnp
from jax import lax
from jax.experimental import pallas as pl
from jax.experimental.pallas import tpu as pltpu
from jax.sharding import PartitionSpec as P

NHYP = 4
NZ, NY, NX = 8, 4, 4
NODES = [(z, y, x) for z in range(NZ) for y in range(NY) for x in range(NX)]
PLANES = [[z * NY * NX + i for i in range(NY * NX)] for z in range(NZ)]
VMEM = pl.BlockSpec(memory_space=pltpu.VMEM)
ANY = pl.BlockSpec(memory_space=pl.ANY)
SMEM = pl.BlockSpec(memory_space=pltpu.SMEM)
F32, BF16 = jnp.float32, jnp.bfloat16


def node_id(z, y, x):
    return ((z % NZ) * NY + y % NY) * NX + x % NX


def shift(a, dz=0, dy=0, dx=0):
    perm = [(node_id(z, y, x), node_id(z + dz, y + dy, x + dx)) for z, y, x in NODES]
    return lax.ppermute(a, "node", perm)


def shift_cores(a, first, second):
    perm = []
    for z, y, x in NODES:
        for core, (dz, dy, dx) in enumerate((first, second)):
            perm.append((node_id(z, y, x) * 2 + core, node_id(z + dz, y + dy, x + dx) * 2 + core))
    return lax.ppermute(a, ("node", "row"), perm)


def swap_core(a):
    return lax.ppermute(a, "row", [(0, 1), (1, 0)])


RING = (0, 1, 7, 2, 6, 3, 5, 4)
LINE = (0, 1, 3, 2)


def after(a, *others):
    return lax.optimization_barrier((a, *others))[0]


def ring_steps(a):
    up, down = a, a
    chunks = [a]
    for k in range(1, 5):
        late = yield chunks
        up, down = lax.optimization_barrier((up, down, *late))[:2]
        if k < 4:
            up = shift(up, dz=1)
            down = shift(down, dz=-1)
            chunks = chunks + [up, down]
        else:
            last = jnp.where(lax.axis_index("row") == 0, up, down)
            chunks = chunks + [shift_cores(last, (1, 0, 0), (-1, 0, 0))]
    yield chunks


def ring_z(a, late=()):
    late = dict(late)
    steps = ring_steps(a)
    chunks = next(steps)
    for k in range(1, 5):
        chunks = steps.send(late.get(k, ()))
    return chunks


def plane_first(a):
    return jnp.stack([a] + [shift_cores(a, (0, 0, k), (0, k, 0)) for k in LINE[1:]])


def plane_second(a):
    return [a] + [shift_cores(a, (0, k, 0), (0, 0, k)) for k in LINE[1:]]


LINES = [[z * NY * NX + i for z in range(NZ)] for i in range(NY * NX)]


def exchange(blocks, groups):
    return lax.all_to_all(blocks, "node", 0, 0, axis_index_groups=groups, tiled=True)


def halves(x):
    hi = x.astype(BF16)
    return hi, (x - hi.astype(F32)).astype(BF16)


def dot3(a, b, dims):
    d = functools.partial(
        lax.dot_general, dimension_numbers=(dims, ((), ())), preferred_element_type=F32
    )
    return d(a[0], b[0]) + (d(a[0], b[1]) + d(a[1], b[0]))


NT, NN = ((1,), (1,)), ((1,), (0,))


def call(body, idx, far, near, outs, scratch, copies, flops, name, limit=None):
    outs = [o if hasattr(o, "dtype") else jax.ShapeDtypeStruct(o, F32) for o in outs]
    vmem = sum(a.size * a.dtype.itemsize for a in [*near, *outs])
    vmem += sum(s.dtype.itemsize * functools.reduce(lambda p, q: p * q, s.shape) for s in scratch)
    moved = vmem + sum(a.size * a.dtype.itemsize for a in far)
    return pl.pallas_call(
        body,
        out_shape=outs,
        in_specs=[SMEM] + [ANY] * len(far) + [VMEM] * len(near),
        out_specs=[VMEM] * len(outs),
        scratch_shapes=[*scratch] + [pltpu.SemaphoreType.DMA((copies,))] * (copies > 0),
        cost_estimate=pl.CostEstimate(flops=flops, bytes_accessed=moved // 2, transcendentals=0),
        compiler_params=pltpu.CompilerParams(vmem_limit_bytes=limit or min(56 << 20, 2 * vmem + (8 << 20))),
        name=name,
    )(idx, *far, *near)


def fetch(sems, pairs, first=0):
    copies = [pltpu.make_async_copy(a, b, sems.at[first + i]) for i, (a, b) in enumerate(pairs)]
    for copy in copies:
        copy.start()
    return copies


def wait(copies):
    for copy in copies:
        copy.wait()


def wrap(v, n):
    return lax.rem(v + n, n)


def split_rows(full, core, mine, other):
    h = mine.shape[0]
    mine[...] = full[pl.ds(pl.multiple_of(core * h, 8), h), :]
    other[...] = full[pl.ds(pl.multiple_of((1 - core) * h, 8), h), :]


def turn(a):
    return pltpu.roll(a, a.shape[-1] // 2, axis=a.ndim - 1)


def in_half(shape, core):
    return (lax.broadcasted_iota(jnp.int32, shape, len(shape) - 1) < shape[-1] // 2) == (core == 0)


def plane_at(idx, j, i):
    y, x, core = idx[1], idx[2], idx[3]
    dy = jnp.where(core == 0, LINE[j], LINE[i])
    dx = jnp.where(core == 0, LINE[i], LINE[j])
    return wrap(y - dy, 4) * 4 + wrap(x - dx, 4)


def rows_at(dst, row, n):
    return dst.at[pl.ds(pl.multiple_of(row, 8), n), :]


def line_pairs(chunks, dst, z, first=0):
    n = dst.shape[0] // NZ
    return [
        (chunks[k].at[first : first + n, :], rows_at(dst, wrap(z - RING[k], 8) * n, n)) for k in range(8)
    ]


def take_body(idx, panel, child, got, mask, wide):
    n, half = panel.shape
    w = half // 4
    keep = in_half((n, w), idx[3])
    for m in range(4):
        cols = slice(m * w, (m + 1) * w)
        wide[:, cols] = jnp.where(keep, panel[:, cols], turn(got[:, cols])) * mask[:, cols]
    wide[:, half:] = child[...]


def take_deriv_body(idx, deriv, got, first, second):
    n, half = deriv.shape
    w = half // 4
    keep = in_half((n, w), idx[3])
    for m in range(4):
        cols = slice(m * w, (m + 1) * w)
        moved = jnp.where(keep, deriv[:, cols], turn(got[:, cols]))
        first[m] = moved[:, : w // 2]
        second[m] = turn(moved)[:, : w // 2]


def root_body(idx, *refs):
    rz, rp, mine, other, fz, fp, full, sems = refs[:8], refs[8:12], *refs[12:]
    n = fz.shape[0] // NZ
    pairs = line_pairs(rz, fz, idx[0])
    for j in range(4):
        for i in range(4):
            pairs.append((rp[j].at[i], rows_at(fp, plane_at(idx, j, i) * n, n)))
    wait(fetch(sems, pairs))
    full[...] = dot3(halves(fz[...]), halves(fp[...]), NT)
    split_rows(full, idx[3], mine, other)


def couple_body(idx, *refs):
    zs, sp, mask, mask_z, mine, other, s_all, fz, full, sems = refs[:8], refs[8:12], *refs[12:]
    core = idx[3]
    early = fetch(sems, line_pairs(zs, fz, idx[0], sp[0].shape[2]))
    pairs = []
    for j in range(4):
        for i in range(4):
            pairs.append((sp[j].at[i], s_all.at[:, plane_at(idx, j, i)]))
    late = fetch(sems, pairs, 8)
    wait(early)
    panel = halves(fz[...] * mask[...])
    wait(late)
    s_cols = s_all[...].reshape(fz.shape[1], full.shape[1])
    full[...] = -dot3(panel, halves(s_cols), NN) * mask_z[...]
    h = mine.shape[0]
    first, second = full[:h, :], turn(full[h:, :])
    keep = in_half(first.shape, core)
    mine[...] = jnp.where(keep, first, second)
    other[...] = jnp.where(keep, second, first)


def factor_body(half, idx, *refs):
    zs, wide, add, out, fz, fp, sems = refs[:8], refs[8], refs[9:-4], *refs[-4:]
    n, w = zs[0].shape
    part = w // 2
    cols = slice(half * part, (half + 1) * part)
    cut = wide.shape[1] - w + half * part
    pairs = [(wide.at[:, cut : cut + part], fp)]
    for k in range(8):
        pairs.append((zs[k].at[:, cols], rows_at(fz, wrap(idx[0] - RING[k], 8) * n, n)))
    wait(fetch(sems, pairs))
    term = dot3(halves(fz[...]), halves(fp[...]), NT)
    out[...] = add[0][...] + term if add else term


def finish_body(idx, got, mine, deriv, owner, out):
    block = mine[...] + got[...]
    h = block.shape[0]
    out[:h, :] = block
    sums = jnp.sum(block * deriv[...], axis=0, keepdims=True)
    lane = lax.broadcasted_iota(jnp.int32, sums.shape, 1)
    row = jnp.zeros_like(sums)
    for k in range(NHYP):
        total = jnp.sum(jnp.where(owner[...] == k, sums, 0.0), axis=1, keepdims=True)
        row = jnp.where(lane == k, total, row)
    out[h:, :] = jnp.broadcast_to(row, (8, row.shape[1]))


def merge(dst, rows, zz, core):
    own = lax.div(zz, 4) == core
    m = lax.rem(zz, 4)
    keep = in_half(rows.shape, core) == own
    dst[m] = jnp.where(keep, jnp.where(own, rows, turn(rows)), dst[m])


def window(panel, at, w):
    return halves(panel[:, pl.ds(pl.multiple_of(lax.rem(at, 4) * w, 128), w)])


def subtract(full, first, second, at, panel, core):
    h = first.shape[0] - 8
    a = jnp.concatenate([first[:h, :], turn(first[:h, :])], axis=0)
    b = jnp.concatenate([second[:h, :], turn(second[:h, :])], axis=0)
    low = lax.div(at, 4) == core
    a, b = jnp.where(low, a, b), jnp.where(low, turn(b), turn(a))
    cols = jnp.where(in_half(a.shape, core), a, b)
    full[...] -= dot3(halves(cols), panel, NT)


def child_body(idx, *refs):
    cz, wide, kk, out, hi, lo = refs[:6], *refs[6:]
    z, core = idx[0], idx[3]
    w = hi.shape[1]
    out[...] = kk[...]
    for r in (1, 2, 3):
        first, second = cz[RING.index(r) - 1], cz[RING.index(r + 4) - 1]
        at = wrap(z - r, 8)
        subtract(out, first, second, at, window(wide, at, w), core)
    hi[...], lo[...] = window(wide, z, w)


def last_body(idx, *refs):
    cz, hi, lo, part, mine, other, own, full, cw = refs[:8], *refs[8:]
    z, core = idx[0], idx[3]
    h = cz[0].shape[0] - 8
    n = mine.shape[1] - 8
    w = cw.shape[2]
    full[...] = part[...]
    subtract(full, cz[0], cz[7], z, (hi[...], lo[...]), core)
    total = cz[0][h:, :h]
    for k in range(1, 8):
        total += cz[k][h:, :h]
    for out, which in ((mine, core), (other, 1 - core)):
        rows = full[pl.ds(pl.multiple_of(which * h, 8), h), :].T
        for p in range(16):
            out[p, :n, :] = rows[p * n : (p + 1) * n, :]
            out[p, n:, :] = total
    at = pl.multiple_of(lax.rem(z, 4) * n, 8)
    for k in range(8):
        rows = cz[k][pl.ds(at, n), :]
        rows = jnp.where(z >= 4, turn(rows), rows)
        merge(cw, rows, wrap(z - RING[k], 8), core)
    for m in range(4):
        own[:, m * w : (m + 1) * w] = cw[m]


def rows_body(idx, got, out):
    n = out.shape[0]
    for part in range(4):
        for p in range(16):
            at = (part * 16 + p) * n
            out[:, at : at + n] = got[p, :n, part * n : (part + 1) * n]


def turn_blocks(a, w):
    return jnp.roll(a.reshape(a.shape[0], -1, w), w // 2, axis=2).reshape(a.shape)


def per_device(root_inv_t, child_inv_t, panel_t, deriv_t, pattern, owner):
    node, core = lax.axis_index("node"), lax.axis_index("row")
    z, y, x = node // (NY * NX), lax.rem(node // NX, NY), lax.rem(node, NX)
    plane = lax.rem(node, NY * NX)
    idx = jnp.stack([z, y, x, core]).astype(jnp.int32)
    rr, half = root_inv_t.shape
    rc, half_c = child_inv_t.shape
    sr = 2 * half
    zc = sr // NZ
    width = sr // pattern.shape[0]
    mask_all = jnp.repeat(pattern.astype(F32), width)
    owner_all = jnp.repeat(owner, width)
    mask = lax.dynamic_slice_in_dim(mask_all, core * half, half)
    mask_z = lax.dynamic_slice_in_dim(mask_all, z * zc, zc)
    keep = (lax.iota(jnp.int32, half) % zc < zc // 2) == (core == 0)
    keep_z = keep[:zc]
    owner_z = lax.dynamic_slice_in_dim(owner_all, z * zc, zc)[None, :]
    owner_z = jnp.where(keep_z[None, :], owner_z, turn_blocks(owner_z, zc))

    mask_row = mask[None, :]
    r_first = plane_first(root_inv_t)
    r_p = plane_second(r_first)
    r_z = ring_z(jnp.concatenate([root_inv_t, panel_t], axis=0), {2: [r_first], 3: r_p[1:3], 4: [r_p[3]]})
    mask_other = lax.dynamic_slice_in_dim(mask_all, (1 - core) * half, half)[None, :]
    mask_k = jnp.where(keep[None, :], mask_row, turn_blocks(mask_other, zc))
    (wide_own,) = call(
        take_body,
        idx,
        [],
        [panel_t, child_inv_t, swap_core(panel_t), mask_k],
        [(rc, half + half_c)],
        [],
        0,
        2 * rc * half,
        "take",
    )
    gathered = lax.all_gather(wide_own, "node", axis=0, tiled=True, axis_index_groups=PLANES)
    steps = ring_steps(child_inv_t)
    next(steps)
    k_1 = steps.send([r_z[7]])

    deriv_0 = after(deriv_t, r_z[3], r_z[4])
    first_w, second_w = call(
        take_deriv_body,
        idx,
        [],
        [deriv_0, swap_core(deriv_0)],
        [(4, rc, zc // 2)] * 2,
        [],
        0,
        2 * rc * half,
        "take_deriv",
    )
    send = jnp.concatenate([first_w, second_w], axis=0)
    send = after(send, r_z[7])
    d_z = exchange(send, LINES)
    d_lo = d_z[:4].reshape(4 * rc, zc // 2)
    d_hi = d_z[4:].reshape(4 * rc, zc // 2)
    d_z = jnp.where(
        core == 0, jnp.concatenate([d_lo, d_hi], axis=1), jnp.concatenate([d_hi, d_lo], axis=1)
    )

    mine, other = call(
        root_body,
        idx,
        [*r_z, *r_p],
        [],
        [(NZ * rr // 2, zc)] * 2,
        [pltpu.VMEM((NZ * rr, half), F32), pltpu.VMEM((16 * rr, half), F32), pltpu.VMEM((NZ * rr, zc), F32)],
        24,
        6 * NZ * rr * 16 * rr * half,
        "root_cov",
        60 << 20,
    )
    s_own = (mine + swap_core(other)).reshape(4, rr, zc)
    s_first = plane_first(s_own)
    s_first = after(s_first, k_1[1], k_1[2])
    s_p = plane_second(s_first)
    k_2 = steps.send([])
    s_p[1] = after(s_p[1], k_2[3], k_2[4])

    mine, other, s_all = call(
        couple_body,
        idx,
        [*r_z, *s_p],
        [mask_row, mask_z[None, :]],
        [(NZ * rc // 2, zc)] * 2 + [(4, 16, rr, zc)],
        [pltpu.VMEM((NZ * rc, half), F32), pltpu.VMEM((NZ * rc, zc), F32)],
        24,
        6 * NZ * rc * half * zc,
        "coupling",
        60 << 20,
    )
    (c_own,) = call(
        finish_body,
        idx,
        [],
        [swap_core(other), mine, d_z, owner_z],
        [(4 * rc + 8, zc)],
        [],
        0,
        4 * 4 * rc * zc,
        "coupling_sum",
    )
    k_3 = steps.send([])
    c_own = after(c_own, k_3[5], k_3[6])
    k_z = steps.send([])
    wide = after(gathered, c_own)

    kk = []
    for part in range(2):
        kk = call(
            functools.partial(factor_body, part),
            idx,
            [*k_z, wide],
            kk,
            [(NZ * rc, 16 * rc)],
            [pltpu.VMEM((NZ * rc, half_c // 2), F32), pltpu.VMEM((16 * rc, half_c // 2), F32)],
            9,
            3 * NZ * rc * 16 * rc * half_c,
            "factor",
            60 << 20,
        )
        if part == 0:
            (kk_first,) = kk
    (kk,) = kk
    root_cov = after(s_all, c_own).reshape(half, zc)
    root_cov = lax.dynamic_slice_in_dim(root_cov, plane * rr, rr, axis=1).T
    c_z = ring_z(c_own, {2: [root_cov], 3: [kk_first], 4: [kk]})
    part, p_hi, p_lo = call(
        child_body,
        idx,
        [],
        [*c_z[1:7], wide, kk],
        [(NZ * rc, 16 * rc)] + [jax.ShapeDtypeStruct((16 * rc, zc), BF16)] * 2,
        [],
        0,
        6 * 16 * rc * 3 * rc * sr,
        "child_most",
    )
    mine, other, c_rows = call(
        last_body,
        idx,
        [],
        [*c_z, p_hi, p_lo, part],
        [(16, rc + 8, 4 * rc)] * 2 + [(rc, half)],
        [pltpu.VMEM((NZ * rc, 16 * rc), F32), pltpu.VMEM((4, rc, zc), F32)],
        0,
        6 * 16 * rc * rc * sr,
        "child_last",
    )

    block = mine + swap_core(other)
    got = exchange(block, PLANES)
    grad = 2.0 * jnp.sum(got[:, rc, :NHYP], axis=0)
    (child_cov,) = call(rows_body, idx, [], [got], [(rc, half_c)], [], 0, rc * half_c, "child_rows")

    coupling = jnp.where(keep[None, :], c_rows, turn_blocks(swap_core(c_rows), zc))
    return (root_cov, coupling, child_cov, grad)


def solution(mesh):
    placed = (P("node", "row"), P("node", "row"), P("node", "row"), P("node", "row"), P(), P())
    return jax.shard_map(
        per_device,
        mesh=mesh,
        in_specs=placed,
        out_specs=(P("node", "row"), P("node", "row"), P("node", "row"), P()),
        check_vma=False,
    )
```

```python
import functools

import jax
import jax.numpy as jnp
from jax import lax
from jax.experimental import pallas as pl
from jax.experimental.pallas import tpu as pltpu
from jax.sharding import PartitionSpec as P

NHYP = 4
NZ, NY, NX = 8, 4, 4
NODES = [(z, y, x) for z in range(NZ) for y in range(NY) for x in range(NX)]
PLANES = [[z * NY * NX + i for i in range(NY * NX)] for z in range(NZ)]
VMEM = pl.BlockSpec(memory_space=pltpu.VMEM)
ANY = pl.BlockSpec(memory_space=pl.ANY)
SMEM = pl.BlockSpec(memory_space=pltpu.SMEM)
F32, BF16 = jnp.float32, jnp.bfloat16


def node_id(z, y, x):
    return ((z % NZ) * NY + y % NY) * NX + x % NX


def shift(a, dz=0, dy=0, dx=0):
    perm = [(node_id(z, y, x), node_id(z + dz, y + dy, x + dx)) for z, y, x in NODES]
    return lax.ppermute(a, "node", perm)


def shift_cores(a, first, second):
    perm = []
    for z, y, x in NODES:
        for core, (dz, dy, dx) in enumerate((first, second)):
            perm.append((node_id(z, y, x) * 2 + core, node_id(z + dz, y + dy, x + dx) * 2 + core))
    return lax.ppermute(a, ("node", "row"), perm)


def swap_core(a):
    return lax.ppermute(a, "row", [(0, 1), (1, 0)])


RING = (0, 1, 7, 2, 6, 3, 5, 4)
LINE = (0, 1, 3, 2)


def after(a, *others):
    return lax.optimization_barrier((a, *others))[0]


def ring_steps(a):
    up, down = a, a
    chunks = [a]
    for k in range(1, 5):
        late = yield chunks
        up, down = lax.optimization_barrier((up, down, *late))[:2]
        if k < 4:
            up = shift(up, dz=1)
            down = shift(down, dz=-1)
            chunks = chunks + [up, down]
        else:
            last = jnp.where(lax.axis_index("row") == 0, up, down)
            chunks = chunks + [shift_cores(last, (1, 0, 0), (-1, 0, 0))]
    yield chunks


def ring_z(a, late=()):
    late = dict(late)
    steps = ring_steps(a)
    chunks = next(steps)
    for k in range(1, 5):
        chunks = steps.send(late.get(k, ()))
    return chunks


def plane_first(a):
    return jnp.stack([a] + [shift_cores(a, (0, 0, k), (0, k, 0)) for k in LINE[1:]])


def plane_second(a):
    return [a] + [shift_cores(a, (0, k, 0), (0, 0, k)) for k in LINE[1:]]


LINES = [[z * NY * NX + i for z in range(NZ)] for i in range(NY * NX)]


def exchange(blocks, groups):
    return lax.all_to_all(blocks, "node", 0, 0, axis_index_groups=groups, tiled=True)


def halves(x):
    hi = x.astype(BF16)
    return hi, (x - hi.astype(F32)).astype(BF16)


def dot3(a, b, dims):
    d = functools.partial(
        lax.dot_general, dimension_numbers=(dims, ((), ())), preferred_element_type=F32
    )
    return d(a[0], b[0]) + (d(a[0], b[1]) + d(a[1], b[0]))


NT, NN = ((1,), (1,)), ((1,), (0,))


def call(body, idx, far, near, outs, scratch, copies, flops, name, limit=None):
    outs = [o if hasattr(o, "dtype") else jax.ShapeDtypeStruct(o, F32) for o in outs]
    vmem = sum(a.size * a.dtype.itemsize for a in [*near, *outs])
    vmem += sum(s.dtype.itemsize * functools.reduce(lambda p, q: p * q, s.shape) for s in scratch)
    moved = vmem + sum(a.size * a.dtype.itemsize for a in far)
    return pl.pallas_call(
        body,
        out_shape=outs,
        in_specs=[SMEM] + [ANY] * len(far) + [VMEM] * len(near),
        out_specs=[VMEM] * len(outs),
        scratch_shapes=[*scratch] + [pltpu.SemaphoreType.DMA((copies,))] * (copies > 0),
        cost_estimate=pl.CostEstimate(flops=flops, bytes_accessed=moved // 2, transcendentals=0),
        compiler_params=pltpu.CompilerParams(vmem_limit_bytes=limit or min(56 << 20, 2 * vmem + (8 << 20))),
        name=name,
    )(idx, *far, *near)


def fetch(sems, pairs, first=0):
    copies = [pltpu.make_async_copy(a, b, sems.at[first + i]) for i, (a, b) in enumerate(pairs)]
    for copy in copies:
        copy.start()
    return copies


def wait(copies):
    for copy in copies:
        copy.wait()


def wrap(v, n):
    return lax.rem(v + n, n)


def split_rows(full, core, mine, other):
    h = mine.shape[0]
    mine[...] = full[pl.ds(pl.multiple_of(core * h, 8), h), :]
    other[...] = full[pl.ds(pl.multiple_of((1 - core) * h, 8), h), :]


def turn(a):
    return pltpu.roll(a, a.shape[-1] // 2, axis=a.ndim - 1)


def in_half(shape, core):
    return (lax.broadcasted_iota(jnp.int32, shape, len(shape) - 1) < shape[-1] // 2) == (core == 0)


def plane_at(idx, j, i):
    y, x, core = idx[1], idx[2], idx[3]
    dy = jnp.where(core == 0, LINE[j], LINE[i])
    dx = jnp.where(core == 0, LINE[i], LINE[j])
    return wrap(y - dy, 4) * 4 + wrap(x - dx, 4)


def rows_at(dst, row, n):
    return dst.at[pl.ds(pl.multiple_of(row, 8), n), :]


def line_pairs(chunks, dst, z, first=0):
    n = dst.shape[0] // NZ
    return [
        (chunks[k].at[first : first + n, :], rows_at(dst, wrap(z - RING[k], 8) * n, n)) for k in range(8)
    ]


def take_body(idx, panel, child, got, mask, wide):
    n, half = panel.shape
    w = half // 4
    keep = in_half((n, w), idx[3])
    for m in range(4):
        cols = slice(m * w, (m + 1) * w)
        wide[:, cols] = jnp.where(keep, panel[:, cols], turn(got[:, cols])) * mask[:, cols]
    wide[:, half:] = child[...]


def take_deriv_body(idx, deriv, got, first, second):
    n, half = deriv.shape
    w = half // 4
    keep = in_half((n, w), idx[3])
    for m in range(4):
        cols = slice(m * w, (m + 1) * w)
        moved = jnp.where(keep, deriv[:, cols], turn(got[:, cols]))
        first[m] = moved[:, : w // 2]
        second[m] = turn(moved)[:, : w // 2]


def root_body(idx, *refs):
    rz, rp, mine, other, fz, fp, full, sems = refs[:8], refs[8:12], *refs[12:]
    n = fz.shape[0] // NZ
    pairs = line_pairs(rz, fz, idx[0])
    for j in range(4):
        for i in range(4):
            pairs.append((rp[j].at[i], rows_at(fp, plane_at(idx, j, i) * n, n)))
    wait(fetch(sems, pairs))
    full[...] = dot3(halves(fz[...]), halves(fp[...]), NT)
    split_rows(full, idx[3], mine, other)


def couple_body(idx, *refs):
    zs, sp, mask, mask_z, mine, other, s_all, fz, full, sems = refs[:8], refs[8:12], *refs[12:]
    core = idx[3]
    early = fetch(sems, line_pairs(zs, fz, idx[0], sp[0].shape[2]))
    pairs = []
    for j in range(4):
        for i in range(4):
            pairs.append((sp[j].at[i], s_all.at[:, plane_at(idx, j, i)]))
    late = fetch(sems, pairs, 8)
    wait(early)
    panel = halves(fz[...] * mask[...])
    wait(late)
    s_cols = s_all[...].reshape(fz.shape[1], full.shape[1])
    full[...] = -dot3(panel, halves(s_cols), NN) * mask_z[...]
    h = mine.shape[0]
    first, second = full[:h, :], turn(full[h:, :])
    keep = in_half(first.shape, core)
    mine[...] = jnp.where(keep, first, second)
    other[...] = jnp.where(keep, second, first)


def factor_body(half, idx, *refs):
    zs, wide, add, out, fz, fp, sems = refs[:8], refs[8], refs[9:-4], *refs[-4:]
    n, w = zs[0].shape
    part = w // 2
    cols = slice(half * part, (half + 1) * part)
    cut = wide.shape[1] - w + half * part
    pairs = [(wide.at[:, cut : cut + part], fp)]
    for k in range(8):
        pairs.append((zs[k].at[:, cols], rows_at(fz, wrap(idx[0] - RING[k], 8) * n, n)))
    wait(fetch(sems, pairs))
    term = dot3(halves(fz[...]), halves(fp[...]), NT)
    out[...] = add[0][...] + term if add else term


def finish_body(idx, got, mine, deriv, owner, out):
    block = mine[...] + got[...]
    h = block.shape[0]
    out[:h, :] = block
    sums = jnp.sum(block * deriv[...], axis=0, keepdims=True)
    lane = lax.broadcasted_iota(jnp.int32, sums.shape, 1)
    row = jnp.zeros_like(sums)
    for k in range(NHYP):
        total = jnp.sum(jnp.where(owner[...] == k, sums, 0.0), axis=1, keepdims=True)
        row = jnp.where(lane == k, total, row)
    out[h:, :] = jnp.broadcast_to(row, (8, row.shape[1]))


def merge(dst, rows, zz, core):
    own = lax.div(zz, 4) == core
    m = lax.rem(zz, 4)
    keep = in_half(rows.shape, core) == own
    dst[m] = jnp.where(keep, jnp.where(own, rows, turn(rows)), dst[m])


def window(panel, at, w):
    return halves(panel[:, pl.ds(pl.multiple_of(lax.rem(at, 4) * w, 128), w)])


def subtract(full, first, second, at, panel, core):
    h = first.shape[0] - 8
    a = jnp.concatenate([first[:h, :], turn(first[:h, :])], axis=0)
    b = jnp.concatenate([second[:h, :], turn(second[:h, :])], axis=0)
    low = lax.div(at, 4) == core
    a, b = jnp.where(low, a, b), jnp.where(low, turn(b), turn(a))
    cols = jnp.where(in_half(a.shape, core), a, b)
    full[...] -= dot3(halves(cols), panel, NT)


def child_body(idx, *refs):
    cz, wide, kk, out, hi, lo = refs[:6], *refs[6:]
    z, core = idx[0], idx[3]
    w = hi.shape[1]
    out[...] = kk[...]
    for r in (1, 2, 3):
        first, second = cz[RING.index(r) - 1], cz[RING.index(r + 4) - 1]
        at = wrap(z - r, 8)
        subtract(out, first, second, at, window(wide, at, w), core)
    hi[...], lo[...] = window(wide, z, w)


def last_body(idx, *refs):
    cz, hi, lo, part, mine, other, own, full, cw = refs[:8], *refs[8:]
    z, core = idx[0], idx[3]
    h = cz[0].shape[0] - 8
    n = mine.shape[1] - 8
    w = cw.shape[2]
    full[...] = part[...]
    subtract(full, cz[0], cz[7], z, (hi[...], lo[...]), core)
    total = cz[0][h:, :h]
    for k in range(1, 8):
        total += cz[k][h:, :h]
    for out, which in ((mine, core), (other, 1 - core)):
        rows = full[pl.ds(pl.multiple_of(which * h, 8), h), :].T
        for p in range(16):
            out[p, :n, :] = rows[p * n : (p + 1) * n, :]
            out[p, n:, :] = total
    at = pl.multiple_of(lax.rem(z, 4) * n, 8)
    for k in range(8):
        rows = cz[k][pl.ds(at, n), :]
        rows = jnp.where(z >= 4, turn(rows), rows)
        merge(cw, rows, wrap(z - RING[k], 8), core)
    for m in range(4):
        own[:, m * w : (m + 1) * w] = cw[m]


def rows_body(idx, got, out):
    n = out.shape[0]
    for part in range(4):
        for p in range(16):
            at = (part * 16 + p) * n
            out[:, at : at + n] = got[p, :n, part * n : (part + 1) * n]


def turn_blocks(a, w):
    return jnp.roll(a.reshape(a.shape[0], -1, w), w // 2, axis=2).reshape(a.shape)


def per_device(root_inv_t, child_inv_t, panel_t, deriv_t, pattern, owner):
    node, core = lax.axis_index("node"), lax.axis_index("row")
    z, y, x = node // (NY * NX), lax.rem(node // NX, NY), lax.rem(node, NX)
    plane = lax.rem(node, NY * NX)
    idx = jnp.stack([z, y, x, core]).astype(jnp.int32)
    rr, half = root_inv_t.shape
    rc, half_c = child_inv_t.shape
    sr = 2 * half
    zc = sr // NZ
    width = sr // pattern.shape[0]
    mask_all = jnp.repeat(pattern.astype(F32), width)
    owner_all = jnp.repeat(owner, width)
    mask = lax.dynamic_slice_in_dim(mask_all, core * half, half)
    mask_z = lax.dynamic_slice_in_dim(mask_all, z * zc, zc)
    keep = (lax.iota(jnp.int32, half) % zc < zc // 2) == (core == 0)
    keep_z = keep[:zc]
    owner_z = lax.dynamic_slice_in_dim(owner_all, z * zc, zc)[None, :]
    owner_z = jnp.where(keep_z[None, :], owner_z, turn_blocks(owner_z, zc))

    mask_row = mask[None, :]
    r_first = plane_first(root_inv_t)
    r_p = plane_second(r_first)
    r_z = ring_z(jnp.concatenate([root_inv_t, panel_t], axis=0), {2: [r_first], 3: r_p[1:3], 4: [r_p[3]]})
    mask_other = lax.dynamic_slice_in_dim(mask_all, (1 - core) * half, half)[None, :]
    mask_k = jnp.where(keep[None, :], mask_row, turn_blocks(mask_other, zc))
    (wide_own,) = call(
        take_body,
        idx,
        [],
        [panel_t, child_inv_t, swap_core(panel_t), mask_k],
        [(rc, half + half_c)],
        [],
        0,
        2 * rc * half,
        "take",
    )
    gathered = lax.all_gather(wide_own, "node", axis=0, tiled=True, axis_index_groups=PLANES)
    steps = ring_steps(child_inv_t)
    next(steps)
    k_1 = steps.send([r_z[7]])

    deriv_0 = after(deriv_t, r_z[3], r_z[4])
    first_w, second_w = call(
        take_deriv_body,
        idx,
        [],
        [deriv_0, swap_core(deriv_0)],
        [(4, rc, zc // 2)] * 2,
        [],
        0,
        2 * rc * half,
        "take_deriv",
    )
    send = jnp.concatenate([first_w, second_w], axis=0)
    send = after(send, r_z[7])
    d_z = exchange(send, LINES)
    d_lo = d_z[:4].reshape(4 * rc, zc // 2)
    d_hi = d_z[4:].reshape(4 * rc, zc // 2)
    d_z = jnp.where(
        core == 0, jnp.concatenate([d_lo, d_hi], axis=1), jnp.concatenate([d_hi, d_lo], axis=1)
    )

    r_p[1] = after(r_p[1], send)
    mine, other = call(
        root_body,
        idx,
        [*r_z, *r_p],
        [],
        [(NZ * rr // 2, zc)] * 2,
        [pltpu.VMEM((NZ * rr, half), F32), pltpu.VMEM((16 * rr, half), F32), pltpu.VMEM((NZ * rr, zc), F32)],
        24,
        6 * NZ * rr * 16 * rr * half,
        "root_cov",
        60 << 20,
    )
    s_own = (mine + swap_core(other)).reshape(4, rr, zc)
    s_first = plane_first(s_own)
    s_first = after(s_first, k_1[1], k_1[2])
    s_p = plane_second(s_first)
    k_2 = steps.send([])
    s_p[1] = after(s_p[1], k_2[3], k_2[4])

    mine, other, s_all = call(
        couple_body,
        idx,
        [*r_z, *s_p],
        [mask_row, mask_z[None, :]],
        [(NZ * rc // 2, zc)] * 2 + [(4, 16, rr, zc)],
        [pltpu.VMEM((NZ * rc, half), F32), pltpu.VMEM((NZ * rc, zc), F32)],
        24,
        6 * NZ * rc * half * zc,
        "coupling",
        60 << 20,
    )
    (c_own,) = call(
        finish_body,
        idx,
        [],
        [swap_core(other), mine, d_z, owner_z],
        [(4 * rc + 8, zc)],
        [],
        0,
        4 * 4 * rc * zc,
        "coupling_sum",
    )
    k_3 = steps.send([])
    c_own = after(c_own, k_3[5], k_3[6])
    k_z = steps.send([])
    wide = after(gathered, c_own)

    kk = []
    for part in range(2):
        kk = call(
            functools.partial(factor_body, part),
            idx,
            [*k_z, wide],
            kk,
            [(NZ * rc, 16 * rc)],
            [pltpu.VMEM((NZ * rc, half_c // 2), F32), pltpu.VMEM((16 * rc, half_c // 2), F32)],
            9,
            3 * NZ * rc * 16 * rc * half_c,
            "factor",
            60 << 20,
        )
        if part == 0:
            (kk_first,) = kk
    (kk,) = kk
    root_cov = after(s_all, c_own).reshape(half, zc)
    root_cov = lax.dynamic_slice_in_dim(root_cov, plane * rr, rr, axis=1).T
    c_z = ring_z(c_own, {2: [root_cov], 3: [kk_first], 4: [kk]})
    part, p_hi, p_lo = call(
        child_body,
        idx,
        [],
        [*c_z[1:7], wide, kk],
        [(NZ * rc, 16 * rc)] + [jax.ShapeDtypeStruct((16 * rc, zc), BF16)] * 2,
        [],
        0,
        6 * 16 * rc * 3 * rc * sr,
        "child_most",
    )
    mine, other, c_rows = call(
        last_body,
        idx,
        [],
        [*c_z, p_hi, p_lo, part],
        [(16, rc + 8, 4 * rc)] * 2 + [(rc, half)],
        [pltpu.VMEM((NZ * rc, 16 * rc), F32), pltpu.VMEM((4, rc, zc), F32)],
        0,
        6 * 16 * rc * rc * sr,
        "child_last",
    )

    block = mine + swap_core(other)
    got = exchange(block, PLANES)
    grad = 2.0 * jnp.sum(got[:, rc, :NHYP], axis=0)
    (child_cov,) = call(rows_body, idx, [], [got], [(rc, half_c)], [], 0, rc * half_c, "child_rows")

    coupling = jnp.where(keep[None, :], c_rows, turn_blocks(swap_core(c_rows), zc))
    return (root_cov, coupling, child_cov, grad)


def solution(mesh):
    placed = (P("node", "row"), P("node", "row"), P("node", "row"), P("node", "row"), P(), P())
    return jax.shard_map(
        per_device,
        mesh=mesh,
        in_specs=placed,
        out_specs=(P("node", "row"), P("node", "row"), P("node", "row"), P()),
        check_vma=False,
    )
```
